512 devices in a mesh: dp: 32 (over y_hi, z), expert: 16 (over y_lo, x, core).
Axes of the slice: x: 4, y: 4 (y_hi: 2, y_lo: 2; y = y_hi * 2 + y_lo), z: 16, core: 2. Of those that a mesh axis runs over, the one named last changes fastest.
Arguments:
- tokens: bfloat16 [65536, 1024], P(('dp', 'expert')), may hold values from -6 to 6
- cotangent: bfloat16 [65536, 1024], P(('dp', 'expert')), may hold values from -6 to 6
- route_experts: int32 [65536, 8], P(('dp', 'expert')), may hold values from 0 to 15, as said below
- route_weights: float32 [65536, 8], P(('dp', 'expert')), may hold values from 0.05 to 0.4
- gate_up: bfloat16 [16, 1024, 768], P('expert', 'dp'), may hold values from -0.1875 to 0.1875
- down: bfloat16 [16, 1024, 384], P('expert', 'dp'), may hold values from -0.3125 to 0.3125
Outputs:
- token_grad: bfloat16 [65536, 1024], P(('dp', 'expert'))
- grad_gate_up: float32 [16, 1024, 768], P('expert', 'dp')
The draws below stay inside these ranges and needn't reach their ends.
Inputs may be any that keep to these rules, and one draw needn't show every extreme that they name: `route_experts`: each token names 8 different experts. Among the rows of one device no expert is named by more than 80 rows, and one expert is named by exactly 80 rows of every device.
All inputs are finite; a program needn't handle non-finite values.
Results may differ from the reference program's by a relative error of at most 0.02.
Values may be sent and summed in bfloat16 or wider, within the bound.
No kernel may reach another device: no remote copies, remote signals or barrier semaphores. Data moves between devices by JAX's collectives and lax.ppermute only.
A program may use at most 64 MiB of HBM per device.

```python
import math
import jax
import jax.numpy as jnp
from jax import lax

D = 1024
FFW = 384
TOPK = 8
TOK_DEV = 128
EXPERTS = 16
CAP = 80
TOKENS = 65536


def draw_route_experts(key, part):
    key = jax.random.fold_in(key, 11)
    block_total = TOKENS // TOK_DEV
    base_count = TOK_DEV // EXPERTS
    step_count = TOK_DEV // (4 * EXPERTS)
    key_label, key_first, key_second, key_rows = jax.random.split(key, 4)
    labels = jax.random.permutation(key_label, EXPERTS).astype(jnp.int32)
    first_move = jax.random.randint(key_first, (block_total,), 0, step_count + 1)
    second_move = jax.random.randint(key_second, (block_total,), 0, step_count + 1)
    halves = jnp.where(jnp.arange(EXPERTS) < TOPK, step_count, -step_count)
    counts = jnp.broadcast_to(base_count + halves, (block_total, EXPERTS)).astype(jnp.int32)
    counts = counts.at[:, 0].add(-first_move).at[:, TOPK - 1].add(first_move)
    counts = counts.at[:, TOPK].add(-second_move).at[:, EXPERTS - 1].add(second_move)

    def one_block(block_counts, block_key):
        bases = jnp.repeat(jnp.arange(EXPERTS, dtype=jnp.int32), block_counts, total_repeat_length=TOK_DEV)
        return jax.random.permutation(block_key, bases)
    block_keys = jax.random.split(key_rows, block_total)
    bases = jax.vmap(one_block)(counts, block_keys)
    offsets = jnp.arange(TOPK, dtype=jnp.int32)
    chosen = (bases[:, :, None] + offsets[None, None, :]) % EXPERTS
    return labels[chosen].reshape(TOKENS, TOPK).astype(jnp.int32)


def steps_of(rng, dims, cuts, low, high):
    def one(position, parts):
        heights = jax.random.uniform(jax.random.fold_in(jax.random.fold_in(rng, 6), position), (parts,), jnp.float32, low / len(cuts), high / len(cuts))
        return jnp.repeat(jnp.exp(heights), dims[position] // parts).reshape((-1,) + (1,) * (len(dims) - position - 1))

    factor_of = one(*cuts[0])
    for cut in cuts[1:]:
        factor_of = factor_of * one(*cut)
    return factor_of


def bell_draw(key, dims, deviation, bound, cuts=(), held_as=jnp.bfloat16):
    array = jax.random.normal(key, dims, jnp.float32) * deviation
    if len(cuts) > 0:
        array = steps_of(key, dims, cuts, -0.22, 0.18) * array
    return jnp.clip(array, min=-bound, max=bound).astype(held_as)


def setup_inputs(seed: int = 0) -> dict:
    key_of = jax.random.split(jax.random.key(seed), 7)
    return {
        "tokens": bell_draw(key_of[0], (TOKENS, D), 1.0, 6.0, ((0, 512),)),
        "cotangent": bell_draw(key_of[1], (TOKENS, D), 1.0, 6.0, ((0, 512),)),
        "route_experts": draw_route_experts(jax.random.fold_in(key_of[6], 71), 0),
        "route_weights": jnp.clip(0.05 + 0.35 * jax.random.uniform(key_of[3], (TOKENS, TOPK), jnp.float32) ** steps_of(key_of[3], (TOKENS, TOPK), ((0, 512),), -0.2, 0.2), 0.05, 0.4),
        "gate_up": bell_draw(key_of[4], (EXPERTS, D, 2 * FFW), D ** -0.5, 0.1875, ((0, 16), (1, 32))),
        "down": bell_draw(key_of[5], (EXPERTS, D, FFW), FFW ** -0.5, 0.3125, ((0, 16), (1, 32))),
    }


def reference(tokens, cotangent, route_experts, route_weights, gate_up, down):
    pair_total = TOKENS * TOPK
    most_rows = TOKENS // TOK_DEV * CAP
    flat_experts = route_experts.reshape(pair_total).astype(jnp.int32)
    flat_weights = route_weights.reshape(pair_total)
    order = jnp.argsort(flat_experts, stable=True).astype(jnp.int32)
    expert_ids = jnp.arange(EXPERTS, dtype=jnp.int32)
    counts = lax.optimization_barrier(jnp.sum((flat_experts[:, None] == expert_ids[None, :]).astype(jnp.int32), axis=0))
    starts = (jnp.cumsum(counts) - counts).astype(jnp.int32)
    grad_scale = 1.0 / math.sqrt(TOKENS)

    def per_expert(totals, expert):
        ranks = jnp.arange(most_rows, dtype=jnp.int32)
        filled = ranks < counts[expert]
        slot_index = jnp.minimum(starts[expert] + ranks, pair_total - 1).astype(jnp.int32)
        pair_index = order[slot_index]
        token_index = (pair_index // TOPK).astype(jnp.int32)
        inputs = tokens[token_index]
        weighted = flat_weights[pair_index][:, None] * cotangent[token_index].astype(jnp.float32)
        cot_rows = jnp.where(filled[:, None], weighted, jnp.zeros_like(weighted)).astype(jnp.bfloat16)
        weights_in = gate_up[expert]
        weights_out = down[expert]
        projected = jnp.dot(inputs, weights_in, preferred_element_type=jnp.float32)
        hidden_grad = jnp.dot(cot_rows, weights_out, preferred_element_type=jnp.float32)
        gate_part = projected[:, :FFW]
        up_part = projected[:, FFW:]
        sigmoid_gate = jax.nn.sigmoid(gate_part)
        grad_gate = hidden_grad * up_part * sigmoid_gate * (1.0 + gate_part * (1.0 - sigmoid_gate))
        grad_up = hidden_grad * gate_part * sigmoid_gate
        pre_grad = jnp.concatenate([grad_gate, grad_up], axis=1).astype(jnp.bfloat16)
        input_grad = jnp.dot(pre_grad, weights_in.T, preferred_element_type=jnp.float32).astype(jnp.bfloat16)
        addend = input_grad.astype(totals.dtype)
        totals = totals.at[token_index].add(jnp.where(filled[:, None], addend, jnp.zeros_like(addend)))
        weight_grad = jnp.dot(inputs.T, pre_grad, preferred_element_type=jnp.float32) * grad_scale
        return (totals, weight_grad)
    totals, weight_grads = lax.scan(per_expert, jnp.zeros((TOKENS, D), jnp.float32), expert_ids)
    return (totals.astype(jnp.bfloat16), weight_grads)
```

```python
import functools
import math

import jax
import jax.numpy as jnp
from jax import lax
from jax.experimental import pallas as pl
from jax.experimental.pallas import tpu as pltpu
from jax.sharding import PartitionSpec as P

EXPERTS = 16
CAP = 80
LANES = 128
RING = 16
NEAR = 4
GROUP = 4
BF16 = jnp.bfloat16
F32 = jnp.float32


def iota(shape, dim):
    return lax.broadcasted_iota(jnp.int32, shape, dim)


def strict_lower(rows):
    return (iota((rows, rows), 0) > iota((rows, rows), 1)).astype(F32).astype(BF16)


def pack_kernel(tok_ref, cot_ref, experts_ref, weights_ref, packed_ref, rank_ref):
    rows, features = tok_ref.shape
    packed_ref[:, :features] = tok_ref[...]
    packed_ref[:, features : 2 * features] = cot_ref[...]
    choices = experts_ref.shape[0]
    label = iota((2 * EXPERTS, rows), 0) % EXPERTS
    dense = jnp.zeros((2 * EXPERTS, rows), F32)
    for k in range(choices):
        dense += jnp.where(experts_ref[k : k + 1, :] == label, weights_ref[k : k + 1, :], 0.0)
    dense = jnp.concatenate([dense, jnp.zeros((LANES - 2 * EXPERTS, rows), F32)], axis=0).T
    high = dense.astype(BF16).astype(F32)
    lane = iota((rows, LANES), 1)
    packed_ref[:, 2 * features :] = jnp.where(lane < EXPERTS, high, dense - high).astype(BF16)
    routed = dense > 0.0
    rank = jnp.dot(
        strict_lower(rows), routed.astype(F32).astype(BF16), preferred_element_type=F32
    )
    rank_ref[...] = jnp.where(routed, rank, 200.0).astype(BF16)


def pack(tokens, cotangent, route_experts, route_weights):
    rows, features = tokens.shape
    return pl.pallas_call(
        pack_kernel,
        out_shape=(
            jax.ShapeDtypeStruct((rows, 2 * features + LANES), BF16),
            jax.ShapeDtypeStruct((rows, LANES), BF16),
        ),
        name="pack_rows",
    )(tokens, cotangent, route_experts.T, route_weights.T)


def expert_kernel(
    my_expert, my_dp, features, hidden, piece_total, g_ref, *refs
):
    pieces = refs[:piece_total]
    row_ref, mine_ref, theirs_ref, weights, inputs, cots, total, sems = refs[piece_total:]
    step = pl.program_id(0)
    expert = my_expert()
    half = features // 2
    dp = my_dp()
    upper = dp // RING
    place = dp % RING
    shard = features // (2 * RING)

    def copies():
        out = []
        for index, (ref, offset, part, source) in enumerate(piece_plan(pieces, shard)):
            spot = (place + offset + RING) % RING
            owner = upper if part == 0 else 1 - upper
            start = pl.multiple_of(owner * half + spot * shard, shard)
            out.append(
                pltpu.make_async_copy(
                    ref.at[pl.ds(source, shard), :], weights.at[pl.ds(start, shard), :], sems.at[index]
                )
            )
        return out

    @pl.when(step == 0)
    def _():
        for copy in copies():
            copy.start()

    rows = g_ref.shape[0] // GROUP
    lane = iota((rows, LANES), 1)
    lower = strict_lower(rows)
    slot_lane = iota((CAP, LANES), 1)
    for s in range(GROUP):
        block = g_ref[s * rows : (s + 1) * rows, :]
        dense = block[:, 2 * features :].astype(F32)
        mine = jnp.sum(jnp.where(lane == expert, dense, 0.0), axis=1, keepdims=True)
        routed = jnp.broadcast_to(mine, (rows, LANES)) > 0.0
        rank = jnp.dot(lower, routed.astype(F32).astype(BF16), preferred_element_type=F32)
        pick = jnp.where(routed & (rank == lane.astype(F32)), 1.0, 0.0).T[:CAP, :].astype(BF16)
        here = pl.ds(s * CAP, CAP)
        inputs[here, :] = jnp.dot(
            pick, block[:, :features], preferred_element_type=F32
        ).astype(BF16)
        chosen = jnp.dot(pick, block[:, 2 * features :], preferred_element_type=F32)
        scale = jnp.sum(
            jnp.where((slot_lane == expert) | (slot_lane == expert + EXPERTS), chosen, 0.0),
            axis=1,
            keepdims=True,
        )
        cots[here, :] = (
            scale
            * jnp.dot(pick, block[:, features : 2 * features], preferred_element_type=F32)
        ).astype(BF16)

    @pl.when(step == 0)
    def _():
        for copy in copies():
            copy.wait()
        total[...] = jnp.zeros_like(total)

    projected = jnp.dot(inputs[...], weights[:, : 2 * hidden], preferred_element_type=F32)
    hidden_grad = jnp.dot(cots[...], weights[:, 2 * hidden :], preferred_element_type=F32)
    gate_part = projected[:, :hidden]
    up_part = projected[:, hidden:]
    sigmoid_gate = jax.nn.sigmoid(gate_part)
    grad_gate = hidden_grad * up_part * sigmoid_gate * (1.0 + gate_part * (1.0 - sigmoid_gate))
    grad_up = hidden_grad * gate_part * sigmoid_gate
    pre_grad = jnp.concatenate([grad_gate, grad_up], axis=1).astype(BF16)
    row_ref[...] = lax.dot_general(
        pre_grad, weights[:, : 2 * hidden], (((1,), (1,)), ((), ())), preferred_element_type=F32
    ).astype(BF16)
    total[...] += lax.dot_general(
        inputs[...], pre_grad, (((0,), (0,)), ((), ())), preferred_element_type=F32
    )

    @pl.when(step == pl.num_programs(0) - 1)
    def _():
        mine_ref[...] = total[pl.ds(pl.multiple_of(upper * half, half), half), :].astype(BF16)
        theirs_ref[...] = total[pl.ds(pl.multiple_of((1 - upper) * half, half), half), :].astype(BF16)


def piece_plan(pieces, shard):
    plan = []
    offsets = [0] + [o for j in range(1, RING // 2) for o in (-j, j)]
    for ref, offset in zip(pieces, offsets):
        plan += [(ref, offset, 0, 0), (ref, offset, 1, shard)]
    far_own, far_other = pieces[len(offsets) :]
    plan += [(far_own, -(RING // 2), 0, 0), (far_other, RING // 2, 1, 0)]
    return plan


def expert_work(gathered, pieces, features, hidden, my_expert, my_dp):
    rows = gathered.shape[0] // EXPERTS
    steps = EXPERTS // GROUP
    half = features // 2
    return pl.pallas_call(
        functools.partial(expert_kernel, my_expert, my_dp, features, hidden, len(pieces)),
        grid=(steps,),
        in_specs=[pl.BlockSpec((GROUP * rows, gathered.shape[1]), lambda i: (i, 0))]
        + [pl.BlockSpec(memory_space=pl.ANY)] * len(pieces),
        out_specs=(
            pl.BlockSpec((GROUP * CAP, features), lambda i: (i, 0)),
            pl.BlockSpec((half, 2 * hidden), lambda i: (0, 0)),
            pl.BlockSpec((half, 2 * hidden), lambda i: (0, 0)),
        ),
        out_shape=(
            jax.ShapeDtypeStruct((EXPERTS * CAP, features), BF16),
            jax.ShapeDtypeStruct((half, 2 * hidden), BF16),
            jax.ShapeDtypeStruct((half, 2 * hidden), BF16),
        ),
        scratch_shapes=[
            pltpu.VMEM((features, 3 * hidden), BF16),
            pltpu.VMEM((GROUP * CAP, features), BF16),
            pltpu.VMEM((GROUP * CAP, features), BF16),
            pltpu.VMEM((features, 2 * hidden), F32),
            pltpu.SemaphoreType.DMA((2 * RING,)),
        ],
        compiler_params=pltpu.CompilerParams(vmem_limit_bytes=48 * 1024 * 1024),
        cost_estimate=pl.CostEstimate(
            flops=8 * EXPERTS * CAP * features * 2 * hidden,
            bytes_accessed=16 * 1024 * 1024,
            transcendentals=EXPERTS * CAP * hidden,
        ),
        name="expert_work",
    )(gathered, *pieces)


def combine_kernel(rank_ref, back_ref, out_ref):
    slots = back_ref.shape[0]
    lanes = rank_ref.shape[1]
    column = iota((lanes, slots), 1) - CAP * iota((lanes, slots), 0)
    spread = ((column >= 0) & (column < CAP)).astype(F32).astype(BF16)
    rank = jnp.dot(rank_ref[...], spread, preferred_element_type=F32)
    slot = iota((1, slots), 1)
    slot = (slot - CAP * ((slot * 3277) >> 18)).astype(F32)
    pick = jnp.where(rank == slot, 1.0, 0.0).astype(BF16)
    out_ref[...] = jnp.dot(pick, back_ref[...], preferred_element_type=F32).astype(BF16)


def combine(rank, back):
    return pl.pallas_call(
        combine_kernel,
        out_shape=jax.ShapeDtypeStruct((rank.shape[0], back.shape[1]), BF16),
        compiler_params=pltpu.CompilerParams(vmem_limit_bytes=32 * 1024 * 1024),
        name="combine_rows",
    )(rank, back)


def swap_halves(x):
    return lax.ppermute(x, "dp", [(d, (d + RING) % (2 * RING)) for d in range(2 * RING)])


def shift_ring(x, by):
    pairs = [(d, d // RING * RING + (d + by) % RING) for d in range(2 * RING)]
    return lax.ppermute(x, "dp", pairs)


def shift_near(x, by):
    pairs = [(d, d // NEAR * NEAR + (d + by) % NEAR) for d in range(2 * RING)]
    return lax.ppermute(x, "dp", pairs)


def gather_weights(gate_up, down):
    own = jnp.concatenate([gate_up[0], down[0]], axis=1)
    shard = own.shape[0]
    both = jnp.concatenate([own, swap_halves(own)], axis=0)
    pieces = [both]
    ahead = behind = both
    for _ in range(1, RING // 2):
        ahead = shift_ring(ahead, 1)
        behind = shift_ring(behind, -1)
        pieces += [ahead, behind]
    return pieces + [shift_ring(ahead[:shard], 1), shift_ring(behind[shard:], -1)]


def scatter_sum(mine, theirs, scale):
    shard = mine.shape[0] // RING
    place = lax.axis_index("dp") % RING
    near, far = place % NEAR, place // NEAR
    part = (mine.astype(F32) + swap_halves(theirs).astype(F32)).astype(BF16)
    part = part.reshape(RING // NEAR, NEAR, shard, -1)

    def column(k):
        return lax.dynamic_index_in_dim(part, k % NEAR, axis=1, keepdims=False)

    total = column(near).astype(F32)
    for by in range(1, NEAR):
        total += shift_near(column(near + by), by).astype(F32)
    part2 = total.astype(BF16)

    def row(k):
        return lax.dynamic_index_in_dim(part2, k % (RING // NEAR), axis=0, keepdims=False)

    total = row(far).astype(F32)
    for by in range(1, RING // NEAR):
        total += shift_ring(row(far + by), by * NEAR).astype(F32)
    return (total * scale)[None]


def shards(tokens, cotangent, route_experts, route_weights, gate_up, down):
    rows, features = tokens.shape
    hidden = down.shape[2]
    packed, rank = pack(tokens, cotangent, route_experts, route_weights)
    gathered = lax.all_gather(packed, "expert", axis=0, tiled=True)
    pieces = gather_weights(gate_up, down)
    row_grads, mine, theirs = expert_work(
        gathered,
        pieces,
        features,
        hidden,
        lambda: lax.axis_index("expert"),
        lambda: lax.axis_index("dp"),
    )
    returned = lax.all_to_all(
        row_grads.reshape(EXPERTS, CAP, features), "expert", split_axis=0, concat_axis=0, tiled=True
    )
    grad_scale = 1.0 / math.sqrt(rows * lax.axis_size("dp") * lax.axis_size("expert"))
    grad_gate_up = scatter_sum(mine, theirs, grad_scale)
    token_grad = combine(rank, returned.reshape(EXPERTS * CAP, features))
    return (token_grad, grad_gate_up)


def solution(mesh):
    in_specs = (
        P(("dp", "expert"), None),
        P(("dp", "expert"), None),
        P(("dp", "expert"), None),
        P(("dp", "expert"), None),
        P("expert", "dp", None),
        P("expert", "dp", None),
    )
    out_specs = (P(("dp", "expert"), None), P("expert", "dp", None))
    return jax.shard_map(shards, mesh=mesh, in_specs=in_specs, out_specs=out_specs, check_vma=False)
```

```python
import functools
import math

import jax
import jax.numpy as jnp
from jax import lax
from jax.experimental import pallas as pl
from jax.experimental.pallas import tpu as pltpu
from jax.sharding import PartitionSpec as P

EXPERTS = 16
CAP = 80
LANES = 128
RING = 16
NEAR = 4
PAIR = 2
BLOCKS = 4
UNROUTED = 200.0
BF16 = jnp.bfloat16
F32 = jnp.float32


def iota(shape, dim):
    return lax.broadcasted_iota(jnp.int32, shape, dim)


def as_bf16(mask):
    return jnp.where(mask, 1.0, 0.0).astype(BF16)


def pack_kernel(tok_ref, cot_ref, experts_ref, weights_ref, packed_ref, rank_ref):
    rows, features = tok_ref.shape
    packed_ref[:, :features] = tok_ref[...]
    packed_ref[:, features : 2 * features] = cot_ref[...]
    label = iota((EXPERTS, rows), 0)
    dense = jnp.zeros((EXPERTS, rows), F32)
    for k in range(experts_ref.shape[0]):
        dense += jnp.where(experts_ref[k : k + 1, :] == label, weights_ref[k : k + 1, :], 0.0)
    routed = dense > 0.0
    before = as_bf16(iota((rows, rows), 0) < iota((rows, rows), 1))
    rank = jnp.dot(as_bf16(routed), before, preferred_element_type=F32)
    rank = jnp.where(routed, rank, UNROUTED).astype(BF16)
    high = dense.astype(BF16)
    low = (dense - high.astype(F32)).astype(BF16)
    rest = jnp.zeros((rows - 3 * EXPERTS, rows), BF16)
    packed_ref[:, 2 * features :] = jnp.concatenate([high, low, rank, rest], axis=0)
    rank_ref[...] = rank


def pack(tokens, cotangent, route_experts, route_weights):
    rows, features = tokens.shape
    return pl.pallas_call(
        pack_kernel,
        out_shape=(
            jax.ShapeDtypeStruct((rows, 2 * features + rows), BF16),
            jax.ShapeDtypeStruct((EXPERTS, rows), BF16),
        ),
        name="pack_rows",
    )(tokens, cotangent, route_experts.T, route_weights.T)


def expert_kernel(my_expert, my_dp, plan, features, hidden, g_ref, *refs):
    piece_total = 5
    pieces = refs[:piece_total]
    pre_ref, gate_up_ref, plus_ref, minus_ref, keep_ref = refs[piece_total : piece_total + 5]
    blocks, weights, inputs, cots, total, block_sems, sems = refs[piece_total + 5 :]
    expert = my_expert()
    dp = my_dp()
    upper = dp // RING
    place = dp % RING
    half = features // 2
    shard = half // RING
    pair_total = blocks.shape[0]
    pair_rows = blocks.shape[1]
    rows = pair_rows // PAIR

    def block_copy(p):
        return pltpu.make_async_copy(
            g_ref.at[pl.ds(p * pair_rows, pair_rows), :], blocks.at[p], block_sems.at[p]
        )

    def first_row(owner, offset):
        return pl.multiple_of(owner * half + ((place + offset + RING) % RING) * shard, shard)

    weight_copies = []
    for array, source, offset in plan:
        for part, owner in ((0, upper), (1, 1 - upper)):
            weight_copies.append(
                pltpu.make_async_copy(
                    pieces[array].at[pl.ds(source + part * shard, shard), :],
                    weights.at[pl.ds(first_row(owner, offset), shard), :],
                    sems.at[len(weight_copies)],
                )
            )
    block_copies = [block_copy(p) for p in range(pair_total)]
    for copy in block_copies[:2] + weight_copies + block_copies[2:]:
        copy.start()

    slot = iota((PAIR * CAP, pair_rows), 0).astype(F32)
    label = iota((3 * EXPERTS, rows), 0)

    def compact(p):
        block_copies[p].wait()
        ranks, scales = [], []
        for s in range(PAIR):
            table = blocks[p, s * rows : s * rows + 3 * EXPERTS, 2 * features :].astype(F32)

            def line(k):
                return jnp.sum(
                    jnp.where(label == expert + k * EXPERTS, table, 0.0), axis=0, keepdims=True
                )

            scales.append(line(0) + line(1))
            ranks.append(line(2) + float(s * CAP))
        hit = slot == jnp.concatenate(ranks, axis=1)
        scale = jnp.sum(
            jnp.where(hit, jnp.concatenate(scales, axis=1), 0.0), axis=1, keepdims=True
        )
        pick = as_bf16(hit)
        here = pl.ds(p * PAIR * CAP, PAIR * CAP)
        inputs[here, :] = jnp.dot(
            pick, blocks[p, :, :features], preferred_element_type=F32
        ).astype(BF16)
        cots[here, :] = (
            scale
            * jnp.dot(pick, blocks[p, :, features : 2 * features], preferred_element_type=F32)
        ).astype(BF16)

    block_rows = inputs.shape[0] // BLOCKS
    for m in range(BLOCKS):
        for p in range(m * pair_total // BLOCKS, (m + 1) * pair_total // BLOCKS):
            compact(p)
        if m == 0:
            for copy in weight_copies:
                copy.wait()
            gate_up_ref[...] = weights[:, : 2 * hidden]
        here = pl.ds(m * block_rows, block_rows)
        projected = jnp.dot(inputs[here, :], weights[:, : 2 * hidden], preferred_element_type=F32)
        hidden_grad = jnp.dot(cots[here, :], weights[:, 2 * hidden :], preferred_element_type=F32)
        gate_part = projected[:, :hidden]
        up_part = projected[:, hidden:]
        sigmoid_gate = jax.nn.sigmoid(gate_part)
        grad_gate = hidden_grad * up_part * sigmoid_gate * (1.0 + gate_part * (1.0 - sigmoid_gate))
        grad_up = hidden_grad * gate_part * sigmoid_gate
        pre_ref[here, :hidden] = grad_gate.astype(BF16)
        pre_ref[here, hidden:] = grad_up.astype(BF16)

    strip = features // BLOCKS
    for c in range(BLOCKS):
        total[c * strip : (c + 1) * strip, :] = lax.dot_general(
            inputs[:, c * strip : (c + 1) * strip],
            pre_ref[...],
            (((0,), (0,)), ((), ())),
            preferred_element_type=F32,
        )

    def put(ref, index, offset):
        for owner in range(2):
            ref[index, owner * shard : (owner + 1) * shard, :] = total[
                pl.ds(first_row(owner, offset), shard), :
            ].astype(BF16)

    for j in range(RING // 4):
        put(plus_ref, j, 2 * j + 1)
        put(minus_ref, j, -(2 * j + 1))
    for j in range(RING // 2):
        put(keep_ref, j, 2 * j)


def expert_work(gathered, pieces, plan, features, hidden, my_expert, my_dp):
    rows = gathered.shape[0] // EXPERTS
    slots = EXPERTS * CAP
    shard = features // (2 * RING)
    hbm = pl.BlockSpec(memory_space=pltpu.HBM)
    return pl.pallas_call(
        functools.partial(expert_kernel, my_expert, my_dp, plan, features, hidden),
        in_specs=[hbm] * (1 + len(pieces)),
        out_shape=(
            jax.ShapeDtypeStruct((slots, 2 * hidden), BF16),
            jax.ShapeDtypeStruct((features, 2 * hidden), BF16),
            jax.ShapeDtypeStruct((RING // 4, 2 * shard, 2 * hidden), BF16),
            jax.ShapeDtypeStruct((RING // 4, 2 * shard, 2 * hidden), BF16),
            jax.ShapeDtypeStruct((RING // 2, 2 * shard, 2 * hidden), BF16),
        ),
        scratch_shapes=[
            pltpu.VMEM((EXPERTS // PAIR, PAIR * rows, gathered.shape[1]), BF16),
            pltpu.VMEM((features, 3 * hidden), BF16),
            pltpu.VMEM((slots, features), BF16),
            pltpu.VMEM((slots, features), BF16),
            pltpu.VMEM((features, 2 * hidden), F32),
            pltpu.SemaphoreType.DMA((EXPERTS // PAIR,)),
            pltpu.SemaphoreType.DMA((2 * RING,)),
        ],
        compiler_params=pltpu.CompilerParams(vmem_limit_bytes=48 * 1024 * 1024),
        cost_estimate=pl.CostEstimate(
            flops=5 * slots * features * 2 * hidden,
            bytes_accessed=16 * 1024 * 1024,
            transcendentals=slots * hidden,
        ),
        name="expert_work",
    )(gathered, *pieces)


def row_kernel(pre_ref, gate_up_ref, out_ref):
    out_ref[...] = lax.dot_general(
        pre_ref[...], gate_up_ref[...], (((1,), (1,)), ((), ())), preferred_element_type=F32
    ).astype(BF16)


def row_gradients(pre_grad, gate_up):
    slots, columns = pre_grad.shape
    features = gate_up.shape[0]
    block = slots // BLOCKS
    return pl.pallas_call(
        row_kernel,
        grid=(BLOCKS,),
        in_specs=[
            pl.BlockSpec((block, columns), lambda i: (i, 0)),
            pl.BlockSpec((features, columns), lambda i: (0, 0)),
        ],
        out_specs=pl.BlockSpec((block, features), lambda i: (i, 0)),
        out_shape=jax.ShapeDtypeStruct((slots, features), BF16),
        compiler_params=pltpu.CompilerParams(vmem_limit_bytes=32 * 1024 * 1024),
        cost_estimate=pl.CostEstimate(
            flops=2 * slots * features * columns,
            bytes_accessed=6 * 1024 * 1024,
            transcendentals=0,
        ),
        name="row_gradients",
    )(pre_grad, gate_up)


def combine_kernel(rank_ref, back_ref, out_ref):
    slots = back_ref.shape[0]
    column = iota((EXPERTS, slots), 1) - CAP * iota((EXPERTS, slots), 0)
    spread = as_bf16((column >= 0) & (column < CAP))
    rank = lax.dot_general(
        rank_ref[...], spread, (((0,), (0,)), ((), ())), preferred_element_type=F32
    )
    slot = iota((1, slots), 1)
    slot = (slot - CAP * ((slot * 3277) >> 18)).astype(F32)
    out_ref[...] = jnp.dot(
        as_bf16(rank == slot), back_ref[...], preferred_element_type=F32
    ).astype(BF16)


def combine(rank, back):
    return pl.pallas_call(
        combine_kernel,
        out_shape=jax.ShapeDtypeStruct((rank.shape[1], back.shape[1]), BF16),
        compiler_params=pltpu.CompilerParams(vmem_limit_bytes=32 * 1024 * 1024),
        name="combine_rows",
    )(rank, back)


def swap_halves(x):
    return lax.ppermute(x, "dp", [(d, (d + RING) % (2 * RING)) for d in range(2 * RING)])


def shift_ring(x, by):
    pairs = [(d, d // RING * RING + (d + by) % RING) for d in range(2 * RING)]
    return lax.ppermute(x, "dp", pairs)


def gather_weights(gate_up, down):
    own = jnp.concatenate([gate_up[0], down[0]], axis=1)
    both = jnp.concatenate([own, swap_halves(own)], axis=0)
    unit = both.shape[0]
    up4, down4, far = shift_ring(both, -4), shift_ring(both, 4), shift_ring(both, 8)
    ahead = jnp.concatenate([both, up4], axis=0)
    behind = jnp.concatenate([both, down4], axis=0)
    ahead = jnp.concatenate([ahead, shift_ring(ahead, -2)], axis=0)
    behind = jnp.concatenate([behind, shift_ring(behind, 2)], axis=0)
    odd_ahead, odd_behind = shift_ring(ahead, -1), shift_ring(behind, 1)
    pieces = [ahead, behind, far, odd_ahead, odd_behind]
    held = [[0, 4, 2, 6], [None, -4, -2, -6], [8], [1, 5, 3, 7], [-1, -5, -3, -7]]
    plan = [
        (array, unit * k, offset)
        for array, offsets in enumerate(held)
        for k, offset in enumerate(offsets)
        if offset is not None
    ]
    return pieces, plan


def first_sum_kernel(keep_ref, plus_ref, minus_ref, up_ref, down_ref, rest_ref):
    def part(k):
        value = keep_ref[k].astype(F32)
        if k < 4:
            value += plus_ref[k].astype(F32)
        if k % 8 == 0 or k > 4:
            value += minus_ref[(8 - k) % 8].astype(F32)
        return value.astype(BF16)

    up_ref[0], up_ref[1] = part(1), part(3)
    down_ref[0], down_ref[1] = part(7), part(5)
    for j in range(4):
        rest_ref[j] = part(2 * j)


def second_sum_kernel(my_dp, rest_ref, up_ref, down_ref, out_ref):
    shard = out_ref.shape[1]
    far = (my_dp() % RING) // NEAR
    groups = RING // NEAR
    for j in range(groups):
        value = rest_ref[j].astype(F32)
        if j < 2:
            value += up_ref[j].astype(F32)
        if j == 0 or j == 3:
            value += down_ref[(4 - j) % 4].astype(F32)
        value = value.astype(BF16)
        target = (far + j) % groups
        out_ref[target] = value[:shard]
        out_ref[groups + target] = value[shard:]


def scatter_sum(plus, minus, keep, scale, my_dp):
    unit, columns = keep.shape[1:]
    got_plus, got_minus = shift_ring(plus, 1), shift_ring(minus, -1)
    piece = jax.ShapeDtypeStruct((2, unit, columns), BF16)
    up, down, rest = pl.pallas_call(
        first_sum_kernel,
        out_shape=(piece, piece, jax.ShapeDtypeStruct((4, unit, columns), BF16)),
        name="first_sum",
    )(keep, got_plus, got_minus)
    got_up, got_down = shift_ring(up, 2), shift_ring(down, -2)
    parts = pl.pallas_call(
        functools.partial(second_sum_kernel, my_dp),
        out_shape=jax.ShapeDtypeStruct((2 * RING // NEAR, unit // 2, columns), BF16),
        name="second_sum",
    )(rest, got_up, got_down)
    groups = [
        [y * RING + far * NEAR + near for y in range(2) for far in range(RING // NEAR)]
        for near in range(NEAR)
    ]
    parts = lax.all_to_all(
        parts, "dp", split_axis=0, concat_axis=0, axis_index_groups=groups, tiled=True
    )
    return jnp.sum(parts.astype(F32), axis=0, keepdims=True) * scale


def shards(tokens, cotangent, route_experts, route_weights, gate_up, down):
    rows, features = tokens.shape
    hidden = down.shape[2]
    packed, rank = pack(tokens, cotangent, route_experts, route_weights)
    gathered = lax.all_gather(packed, "expert", axis=0, tiled=True)
    pieces, plan = gather_weights(gate_up, down)

    def my_dp():
        return lax.axis_index("dp")

    pre_grad, full_gate_up, plus, minus, keep = expert_work(
        gathered, pieces, plan, features, hidden, lambda: lax.axis_index("expert"), my_dp
    )
    row_grads = row_gradients(pre_grad, full_gate_up)
    returned = lax.all_to_all(
        row_grads.reshape(EXPERTS, CAP, features), "expert", split_axis=0, concat_axis=0, tiled=True
    )
    grad_scale = 1.0 / math.sqrt(rows * lax.axis_size("dp") * lax.axis_size("expert"))
    grad_gate_up = scatter_sum(plus, minus, keep, grad_scale, my_dp)
    token_grad = combine(rank, returned.reshape(EXPERTS * CAP, features))
    return (token_grad, grad_gate_up)


def solution(mesh):
    in_specs = (
        P(("dp", "expert"), None),
        P(("dp", "expert"), None),
        P(("dp", "expert"), None),
        P(("dp", "expert"), None),
        P("expert", "dp", None),
        P("expert", "dp", None),
    )
    out_specs = (P(("dp", "expert"), None), P("expert", "dp", None))
    return jax.shard_map(shards, mesh=mesh, in_specs=in_specs, out_specs=out_specs, check_vma=False)
```

```python
import functools
import math

import jax
import jax.numpy as jnp
from jax import lax
from jax.experimental import pallas as pl
from jax.experimental.pallas import tpu as pltpu
from jax.sharding import PartitionSpec as P

EXPERTS = 16
CAP = 80
LANES = 128
RING = 16
NEAR = 4
PAIR = 2
BLOCKS = 4
UNROUTED = 200.0
BF16 = jnp.bfloat16
F32 = jnp.float32


def iota(shape, dim):
    return lax.broadcasted_iota(jnp.int32, shape, dim)


def as_bf16(mask):
    return jnp.where(mask, 1.0, 0.0).astype(BF16)


def pack_kernel(tok_ref, cot_ref, experts_ref, weights_ref, packed_ref, rank_ref):
    rows, features = tok_ref.shape
    packed_ref[:, :features] = tok_ref[...]
    packed_ref[:, features : 2 * features] = cot_ref[...]
    label = iota((EXPERTS, rows), 0)
    dense = jnp.zeros((EXPERTS, rows), F32)
    for k in range(experts_ref.shape[0]):
        dense += jnp.where(experts_ref[k : k + 1, :] == label, weights_ref[k : k + 1, :], 0.0)
    routed = dense > 0.0
    before = as_bf16(iota((rows, rows), 0) < iota((rows, rows), 1))
    rank = jnp.dot(as_bf16(routed), before, preferred_element_type=F32)
    rank = jnp.where(routed, rank, UNROUTED).astype(BF16)
    high = dense.astype(BF16)
    low = (dense - high.astype(F32)).astype(BF16)
    rest = jnp.zeros((rows - 3 * EXPERTS, rows), BF16)
    packed_ref[:, 2 * features :] = jnp.concatenate([high, low, rank, rest], axis=0)
    rank_ref[...] = rank


def pack(tokens, cotangent, route_experts, route_weights):
    rows, features = tokens.shape
    return pl.pallas_call(
        pack_kernel,
        out_shape=(
            jax.ShapeDtypeStruct((rows, 2 * features + rows), BF16),
            jax.ShapeDtypeStruct((EXPERTS, rows), BF16),
        ),
        name="pack_rows",
    )(tokens, cotangent, route_experts.T, route_weights.T)


def expert_kernel(my_expert, my_dp, plan, features, hidden, g_ref, *refs):
    piece_total = 1 + max(array for array, _, _, _ in plan)
    pieces = refs[:piece_total]
    pre_ref, gate_up_ref, plus_ref, minus_ref, keep_ref = refs[piece_total : piece_total + 5]
    blocks, weights, inputs, cots, total, block_sems, sems = refs[piece_total + 5 :]
    expert = my_expert()
    dp = my_dp()
    upper = dp // RING
    place = dp % RING
    half = features // 2
    shard = half // RING
    pair_total = blocks.shape[0]
    pair_rows = blocks.shape[1]
    rows = pair_rows // PAIR

    def block_copy(p):
        return pltpu.make_async_copy(
            g_ref.at[pl.ds(p * pair_rows, pair_rows), :], blocks.at[p], block_sems.at[p]
        )

    def first_row(owner, offset):
        return pl.multiple_of(owner * half + ((place + offset + RING) % RING) * shard, shard)

    weight_copies = []
    for array, source, offset, part in plan:
        owner = upper if part == 0 else 1 - upper
        weight_copies.append(
            pltpu.make_async_copy(
                pieces[array].at[pl.ds(source, shard), :],
                weights.at[pl.ds(first_row(owner, offset), shard), :],
                sems.at[len(weight_copies)],
            )
        )
    block_copies = [block_copy(p) for p in range(pair_total)]
    for copy in block_copies[:2] + weight_copies + block_copies[2:]:
        copy.start()

    slot = iota((PAIR * CAP, pair_rows), 0).astype(F32)
    label = iota((3 * EXPERTS, rows), 0)

    def compact(p):
        block_copies[p].wait()
        ranks, scales = [], []
        for s in range(PAIR):
            table = blocks[p, s * rows : s * rows + 3 * EXPERTS, 2 * features :].astype(F32)

            def line(k):
                return jnp.sum(
                    jnp.where(label == expert + k * EXPERTS, table, 0.0), axis=0, keepdims=True
                )

            scales.append(line(0) + line(1))
            ranks.append(line(2) + float(s * CAP))
        hit = slot == jnp.concatenate(ranks, axis=1)
        scale = jnp.sum(
            jnp.where(hit, jnp.concatenate(scales, axis=1), 0.0), axis=1, keepdims=True
        )
        pick = as_bf16(hit)
        here = pl.ds(p * PAIR * CAP, PAIR * CAP)
        inputs[here, :] = jnp.dot(
            pick, blocks[p, :, :features], preferred_element_type=F32
        ).astype(BF16)
        cots[here, :] = (
            scale
            * jnp.dot(pick, blocks[p, :, features : 2 * features], preferred_element_type=F32)
        ).astype(BF16)

    block_rows = inputs.shape[0] // BLOCKS
    for m in range(BLOCKS):
        for p in range(m * pair_total // BLOCKS, (m + 1) * pair_total // BLOCKS):
            compact(p)
        if m == 0:
            for copy in weight_copies:
                copy.wait()
            gate_up_ref[...] = weights[:, : 2 * hidden]
        here = pl.ds(m * block_rows, block_rows)
        projected = jnp.dot(inputs[here, :], weights[:, : 2 * hidden], preferred_element_type=F32)
        hidden_grad = jnp.dot(cots[here, :], weights[:, 2 * hidden :], preferred_element_type=F32)
        gate_part = projected[:, :hidden]
        up_part = projected[:, hidden:]
        sigmoid_gate = jax.nn.sigmoid(gate_part)
        grad_gate = hidden_grad * up_part * sigmoid_gate * (1.0 + gate_part * (1.0 - sigmoid_gate))
        grad_up = hidden_grad * gate_part * sigmoid_gate
        pre_ref[here, :hidden] = grad_gate.astype(BF16)
        pre_ref[here, hidden:] = grad_up.astype(BF16)

    strip = features // BLOCKS
    for c in range(BLOCKS):
        total[c * strip : (c + 1) * strip, :] = lax.dot_general(
            inputs[:, c * strip : (c + 1) * strip],
            pre_ref[...],
            (((0,), (0,)), ((), ())),
            preferred_element_type=F32,
        )

    def put(ref, index, offset):
        for owner in range(2):
            ref[index, owner * shard : (owner + 1) * shard, :] = total[
                pl.ds(first_row(owner, offset), shard), :
            ].astype(BF16)

    for j in range(RING // 4):
        put(plus_ref, j, 2 * j + 1)
        put(minus_ref, j, -(2 * j + 1))
    for j in range(RING // 2):
        put(keep_ref, j, 2 * j)


def expert_work(gathered, pieces, plan, features, hidden, my_expert, my_dp):
    rows = gathered.shape[0] // EXPERTS
    slots = EXPERTS * CAP
    shard = features // (2 * RING)
    hbm = pl.BlockSpec(memory_space=pltpu.HBM)
    return pl.pallas_call(
        functools.partial(expert_kernel, my_expert, my_dp, plan, features, hidden),
        in_specs=[hbm] * (1 + len(pieces)),
        out_shape=(
            jax.ShapeDtypeStruct((slots, 2 * hidden), BF16),
            jax.ShapeDtypeStruct((features, 2 * hidden), BF16),
            jax.ShapeDtypeStruct((RING // 4, 2 * shard, 2 * hidden), BF16),
            jax.ShapeDtypeStruct((RING // 4, 2 * shard, 2 * hidden), BF16),
            jax.ShapeDtypeStruct((RING // 2, 2 * shard, 2 * hidden), BF16),
        ),
        scratch_shapes=[
            pltpu.VMEM((EXPERTS // PAIR, PAIR * rows, gathered.shape[1]), BF16),
            pltpu.VMEM((features, 3 * hidden), BF16),
            pltpu.VMEM((slots, features), BF16),
            pltpu.VMEM((slots, features), BF16),
            pltpu.VMEM((features, 2 * hidden), F32),
            pltpu.SemaphoreType.DMA((EXPERTS // PAIR,)),
            pltpu.SemaphoreType.DMA((2 * RING,)),
        ],
        compiler_params=pltpu.CompilerParams(vmem_limit_bytes=48 * 1024 * 1024),
        cost_estimate=pl.CostEstimate(
            flops=5 * slots * features * 2 * hidden,
            bytes_accessed=16 * 1024 * 1024,
            transcendentals=slots * hidden,
        ),
        name="expert_work",
    )(gathered, *pieces)


def row_kernel(pre_hbm, gate_up_hbm, out_ref, pre_ref, gate_up_ref, sems):
    copies = [
        pltpu.make_async_copy(gate_up_hbm, gate_up_ref, sems.at[0]),
        pltpu.make_async_copy(pre_hbm, pre_ref, sems.at[1]),
    ]
    for copy in copies:
        copy.start()
    for copy in copies:
        copy.wait()
    block = pre_ref.shape[0] // BLOCKS
    for m in range(BLOCKS):
        here = pl.ds(m * block, block)
        out_ref[here, :] = lax.dot_general(
            pre_ref[here, :],
            gate_up_ref[...],
            (((1,), (1,)), ((), ())),
            preferred_element_type=F32,
        ).astype(BF16)


def row_gradients(pre_grad, gate_up):
    slots, columns = pre_grad.shape
    features = gate_up.shape[0]
    return pl.pallas_call(
        row_kernel,
        in_specs=[pl.BlockSpec(memory_space=pltpu.HBM)] * 2,
        out_shape=jax.ShapeDtypeStruct((slots, features), BF16),
        scratch_shapes=[
            pltpu.VMEM((slots, columns), BF16),
            pltpu.VMEM((features, columns), BF16),
            pltpu.SemaphoreType.DMA((2,)),
        ],
        compiler_params=pltpu.CompilerParams(vmem_limit_bytes=32 * 1024 * 1024),
        cost_estimate=pl.CostEstimate(
            flops=2 * slots * features * columns,
            bytes_accessed=6 * 1024 * 1024,
            transcendentals=0,
        ),
        name="row_gradients",
    )(pre_grad, gate_up)


def combine_kernel(rank_ref, back_ref, out_ref):
    slots = back_ref.shape[0]
    column = iota((EXPERTS, slots), 1) - CAP * iota((EXPERTS, slots), 0)
    spread = as_bf16((column >= 0) & (column < CAP))
    rank = lax.dot_general(
        rank_ref[...], spread, (((0,), (0,)), ((), ())), preferred_element_type=F32
    )
    slot = iota((1, slots), 1)
    slot = (slot - CAP * ((slot * 3277) >> 18)).astype(F32)
    out_ref[...] = jnp.dot(
        as_bf16(rank == slot), back_ref[...], preferred_element_type=F32
    ).astype(BF16)


def combine(rank, back):
    return pl.pallas_call(
        combine_kernel,
        out_shape=jax.ShapeDtypeStruct((rank.shape[1], back.shape[1]), BF16),
        compiler_params=pltpu.CompilerParams(vmem_limit_bytes=32 * 1024 * 1024),
        name="combine_rows",
    )(rank, back)


def swap_halves(x):
    return lax.ppermute(x, "dp", [(d, (d + RING) % (2 * RING)) for d in range(2 * RING)])


def shift_ring(x, by):
    pairs = [(d, d // RING * RING + (d + by) % RING) for d in range(2 * RING)]
    return lax.ppermute(x, "dp", pairs)


def gather_weights(gate_up, down):
    own = jnp.concatenate([gate_up[0], down[0]], axis=1)
    shard = own.shape[0]
    ahead = behind = jnp.concatenate([own, swap_halves(own)], axis=0)
    pieces = [ahead]
    plan = [(0, 0, 0, 0), (0, shard, 0, 1)]
    for j in range(1, RING // 2):
        ahead, behind = shift_ring(ahead, 1), shift_ring(behind, -1)
        for piece, offset in ((ahead, -j), (behind, j)):
            plan += [(len(pieces), part * shard, offset, part) for part in range(2)]
            pieces.append(piece)
    plan += [(len(pieces), 0, RING // 2, 0), (len(pieces) + 1, 0, RING // 2, 1)]
    pieces += [shift_ring(ahead[:shard], 1), shift_ring(behind[shard:], -1)]
    return pieces, plan


def first_sum_kernel(keep_ref, plus_ref, minus_ref, up_ref, down_ref, rest_ref):
    def part(k):
        value = keep_ref[k].astype(F32)
        if k < 4:
            value += plus_ref[k].astype(F32)
        if k % 8 == 0 or k > 4:
            value += minus_ref[(8 - k) % 8].astype(F32)
        return value.astype(BF16)

    up_ref[0], up_ref[1] = part(1), part(3)
    down_ref[0], down_ref[1] = part(7), part(5)
    for j in range(4):
        rest_ref[j] = part(2 * j)


def second_sum_kernel(my_dp, rest_ref, up_ref, down_ref, later_ref, out_ref):
    del later_ref
    shard = out_ref.shape[1]
    far = (my_dp() % RING) // NEAR
    groups = RING // NEAR
    for j in range(groups):
        value = rest_ref[j].astype(F32)
        if j < 2:
            value += up_ref[j].astype(F32)
        if j == 0 or j == 3:
            value += down_ref[(4 - j) % 4].astype(F32)
        value = value.astype(BF16)
        target = (far + j) % groups
        out_ref[target] = value[:shard]
        out_ref[groups + target] = value[shard:]


def scatter_sum(plus, minus, keep, later, scale, my_dp):
    unit, columns = keep.shape[1:]
    got_plus, got_minus = shift_ring(plus, 1), shift_ring(minus, -1)
    piece = jax.ShapeDtypeStruct((2, unit, columns), BF16)
    up, down, rest = pl.pallas_call(
        first_sum_kernel,
        out_shape=(piece, piece, jax.ShapeDtypeStruct((4, unit, columns), BF16)),
        name="first_sum",
    )(keep, got_plus, got_minus)
    got_up, got_down = shift_ring(up, 2), shift_ring(down, -2)
    parts = pl.pallas_call(
        functools.partial(second_sum_kernel, my_dp),
        out_shape=jax.ShapeDtypeStruct((2 * RING // NEAR, unit // 2, columns), BF16),
        in_specs=[pl.BlockSpec(memory_space=pltpu.VMEM)] * 3
        + [pl.BlockSpec(memory_space=pltpu.HBM)],
        name="second_sum",
    )(rest, got_up, got_down, later)
    groups = [
        [y * RING + far * NEAR + near for y in range(2) for far in range(RING // NEAR)]
        for near in range(NEAR)
    ]
    parts = lax.all_to_all(
        parts, "dp", split_axis=0, concat_axis=0, axis_index_groups=groups, tiled=True
    )
    return jnp.sum(parts.astype(F32), axis=0, keepdims=True) * scale


def shards(tokens, cotangent, route_experts, route_weights, gate_up, down):
    rows, features = tokens.shape
    hidden = down.shape[2]
    packed, rank = pack(tokens, cotangent, route_experts, route_weights)
    gathered = lax.all_gather(packed, "expert", axis=0, tiled=True)
    pieces, plan = gather_weights(gate_up, down)

    def my_dp():
        return lax.axis_index("dp")

    pre_grad, full_gate_up, plus, minus, keep = expert_work(
        gathered, pieces, plan, features, hidden, lambda: lax.axis_index("expert"), my_dp
    )
    row_grads = row_gradients(pre_grad, full_gate_up)
    returned = lax.all_to_all(
        row_grads.reshape(EXPERTS, CAP, features), "expert", split_axis=0, concat_axis=0, tiled=True
    )
    grad_scale = 1.0 / math.sqrt(rows * lax.axis_size("dp") * lax.axis_size("expert"))
    grad_gate_up = scatter_sum(plus, minus, keep, returned, grad_scale, my_dp)
    token_grad = combine(rank, returned.reshape(EXPERTS * CAP, features))
    return (token_grad, grad_gate_up)


def solution(mesh):
    in_specs = (
        P(("dp", "expert"), None),
        P(("dp", "expert"), None),
        P(("dp", "expert"), None),
        P(("dp", "expert"), None),
        P("expert", "dp", None),
        P("expert", "dp", None),
    )
    out_specs = (P(("dp", "expert"), None), P("expert", "dp", None))
    return jax.shard_map(shards, mesh=mesh, in_specs=in_specs, out_specs=out_specs, check_vma=False)
```

```python
import functools
import math

import jax
import jax.numpy as jnp
from jax import lax
from jax.experimental import pallas as pl
from jax.experimental.pallas import tpu as pltpu
from jax.sharding import PartitionSpec as P

EXPERTS = 16
CAP = 80
LANES = 128
RING = 16
NEAR = 4
PAIR = 2
BLOCKS = 4
UNROUTED = 200.0
BF16 = jnp.bfloat16
F32 = jnp.float32


def iota(shape, dim):
    return lax.broadcasted_iota(jnp.int32, shape, dim)


def as_bf16(mask):
    return jnp.where(mask, 1.0, 0.0).astype(BF16)


def pack_kernel(tok_ref, cot_ref, experts_ref, weights_ref, packed_ref, rank_ref):
    rows, features = tok_ref.shape
    packed_ref[:, :features] = tok_ref[...]
    packed_ref[:, features : 2 * features] = cot_ref[...]
    label = iota((EXPERTS, rows), 0)
    dense = jnp.zeros((EXPERTS, rows), F32)
    for k in range(experts_ref.shape[0]):
        dense += jnp.where(experts_ref[k : k + 1, :] == label, weights_ref[k : k + 1, :], 0.0)
    routed = dense > 0.0
    before = as_bf16(iota((rows, rows), 0) < iota((rows, rows), 1))
    rank = jnp.dot(as_bf16(routed), before, preferred_element_type=F32)
    rank = jnp.where(routed, rank, UNROUTED).astype(BF16)
    high = dense.astype(BF16)
    low = (dense - high.astype(F32)).astype(BF16)
    rest = jnp.zeros((rows - 3 * EXPERTS, rows), BF16)
    packed_ref[:, 2 * features :] = jnp.concatenate([high, low, rank, rest], axis=0)
    rank_ref[...] = rank


def pack(tokens, cotangent, route_experts, route_weights):
    rows, features = tokens.shape
    return pl.pallas_call(
        pack_kernel,
        out_shape=(
            jax.ShapeDtypeStruct((rows, 2 * features + rows), BF16),
            jax.ShapeDtypeStruct((EXPERTS, rows), BF16),
        ),
        compiler_params=pltpu.CompilerParams(vmem_limit_bytes=8 * 1024 * 1024),
        name="pack_rows",
    )(tokens, cotangent, route_experts.T, route_weights.T)


def expert_kernel(my_expert, my_dp, plan, features, hidden, g_ref, *refs):
    piece_total = 1 + max(array for array, _, _, _ in plan)
    pieces = refs[:piece_total]
    row_ref, keep_ref, plus_ref, minus_ref, plus2_ref, minus2_ref = refs[piece_total : piece_total + 6]
    blocks, weights, inputs, cots, pre_grad, row_grad, total = refs[piece_total + 6 : -3]
    block_sems, sems, row_sems = refs[-3:]
    expert = my_expert()
    dp = my_dp()
    upper = dp // RING
    place = dp % RING
    half = features // 2
    shard = half // RING
    pair_total = blocks.shape[0]
    pair_rows = blocks.shape[1]
    rows = pair_rows // PAIR

    def block_copy(p):
        return pltpu.make_async_copy(
            g_ref.at[pl.ds(p * pair_rows, pair_rows), :], blocks.at[p], block_sems.at[p]
        )

    def first_row(owner, offset):
        return pl.multiple_of(owner * half + ((place + offset + RING) % RING) * shard, shard)

    weight_copies = []
    for array, source, offset, part in plan:
        owner = upper if part == 0 else 1 - upper
        weight_copies.append(
            pltpu.make_async_copy(
                pieces[array].at[pl.ds(source, shard), :],
                weights.at[pl.ds(first_row(owner, offset), shard), :],
                sems.at[len(weight_copies)],
            )
        )
    block_copies = [block_copy(p) for p in range(pair_total)]
    for copy in block_copies[:2] + weight_copies + block_copies[2:]:
        copy.start()

    slot = iota((PAIR * CAP, pair_rows), 0).astype(F32)
    label = iota((3 * EXPERTS, rows), 0)

    def compact(p):
        block_copies[p].wait()
        ranks, scales = [], []
        for s in range(PAIR):
            table = blocks[p, s * rows : s * rows + 3 * EXPERTS, 2 * features :].astype(F32)

            def line(k):
                return jnp.sum(
                    jnp.where(label == expert + k * EXPERTS, table, 0.0), axis=0, keepdims=True
                )

            scales.append(line(0) + line(1))
            ranks.append(line(2) + float(s * CAP))
        hit = slot == jnp.concatenate(ranks, axis=1)
        scale = jnp.sum(
            jnp.where(hit, jnp.concatenate(scales, axis=1), 0.0), axis=1, keepdims=True
        )
        pick = as_bf16(hit)
        here = pl.ds(p * PAIR * CAP, PAIR * CAP)
        inputs[here, :] = jnp.dot(
            pick, blocks[p, :, :features], preferred_element_type=F32
        ).astype(BF16)
        cots[here, :] = (
            scale
            * jnp.dot(pick, blocks[p, :, features : 2 * features], preferred_element_type=F32)
        ).astype(BF16)

    block_rows = inputs.shape[0] // BLOCKS
    row_copies = []
    for m in range(BLOCKS):
        for p in range(m * pair_total // BLOCKS, (m + 1) * pair_total // BLOCKS):
            compact(p)
        if m == 0:
            for copy in weight_copies:
                copy.wait()
        here = pl.ds(m * block_rows, block_rows)
        projected = jnp.dot(inputs[here, :], weights[:, : 2 * hidden], preferred_element_type=F32)
        hidden_grad = jnp.dot(cots[here, :], weights[:, 2 * hidden :], preferred_element_type=F32)
        gate_part = projected[:, :hidden]
        up_part = projected[:, hidden:]
        sigmoid_gate = jax.nn.sigmoid(gate_part)
        grad_gate = hidden_grad * up_part * sigmoid_gate * (1.0 + gate_part * (1.0 - sigmoid_gate))
        grad_up = hidden_grad * gate_part * sigmoid_gate
        pre_grad[here, :hidden] = grad_gate.astype(BF16)
        pre_grad[here, hidden:] = grad_up.astype(BF16)
        row_grad[here, :] = lax.dot_general(
            pre_grad[here, :],
            weights[:, : 2 * hidden],
            (((1,), (1,)), ((), ())),
            preferred_element_type=F32,
        ).astype(BF16)
        row_copies.append(
            pltpu.make_async_copy(row_grad.at[here, :], row_ref.at[here, :], row_sems.at[m])
        )
        row_copies[m].start()

    strip = features // BLOCKS
    for c in range(BLOCKS):
        total[c * strip : (c + 1) * strip, :] = lax.dot_general(
            inputs[:, c * strip : (c + 1) * strip],
            pre_grad[...],
            (((0,), (0,)), ((), ())),
            preferred_element_type=F32,
        )

    def part(owner, offset):
        return total[pl.ds(first_row(owner, offset), shard), :].astype(BF16)

    for j in range(RING // NEAR):
        for ref, offset in ((keep_ref, 0), (plus_ref, 1), (minus_ref, -1)):
            for owner in range(2):
                ref[j, owner * shard : (owner + 1) * shard, :] = part(owner, NEAR * j + offset)
        plus2_ref[j] = part(0, NEAR * j + 2)
        minus2_ref[j] = part(1, NEAR * j + 2)
    for copy in row_copies:
        copy.wait()


def expert_work(gathered, pieces, plan, features, hidden, my_expert, my_dp):
    rows = gathered.shape[0] // EXPERTS
    slots = EXPERTS * CAP
    shard = features // (2 * RING)
    hbm = pl.BlockSpec(memory_space=pltpu.HBM)
    whole = jax.ShapeDtypeStruct((RING // NEAR, 2 * shard, 2 * hidden), BF16)
    half = jax.ShapeDtypeStruct((RING // NEAR, shard, 2 * hidden), BF16)
    return pl.pallas_call(
        functools.partial(expert_kernel, my_expert, my_dp, plan, features, hidden),
        in_specs=[hbm] * (1 + len(pieces)),
        out_shape=(
            jax.ShapeDtypeStruct((slots, features), BF16),
            whole,
            whole,
            whole,
            half,
            half,
        ),
        out_specs=(hbm,) + (pl.BlockSpec(memory_space=pltpu.VMEM),) * 5,
        scratch_shapes=[
            pltpu.VMEM((EXPERTS // PAIR, PAIR * rows, gathered.shape[1]), BF16),
            pltpu.VMEM((features, 3 * hidden), BF16),
            pltpu.VMEM((slots, features), BF16),
            pltpu.VMEM((slots, features), BF16),
            pltpu.VMEM((slots, 2 * hidden), BF16),
            pltpu.VMEM((slots, features), BF16),
            pltpu.VMEM((features, 2 * hidden), F32),
            pltpu.SemaphoreType.DMA((EXPERTS // PAIR,)),
            pltpu.SemaphoreType.DMA((2 * RING,)),
            pltpu.SemaphoreType.DMA((BLOCKS,)),
        ],
        compiler_params=pltpu.CompilerParams(vmem_limit_bytes=48 * 1024 * 1024),
        cost_estimate=pl.CostEstimate(
            flops=7 * slots * features * 2 * hidden,
            bytes_accessed=16 * 1024 * 1024,
            transcendentals=slots * hidden,
        ),
        name="expert_work",
    )(gathered, *pieces)


def combine_kernel(rank_ref, back_ref, out_ref):
    slots = back_ref.shape[0]
    column = iota((EXPERTS, slots), 1) - CAP * iota((EXPERTS, slots), 0)
    spread = as_bf16((column >= 0) & (column < CAP))
    rank = lax.dot_general(
        rank_ref[...], spread, (((0,), (0,)), ((), ())), preferred_element_type=F32
    )
    slot = iota((1, slots), 1)
    slot = (slot - CAP * ((slot * 3277) >> 18)).astype(F32)
    out_ref[...] = jnp.dot(
        as_bf16(rank == slot), back_ref[...], preferred_element_type=F32
    ).astype(BF16)


def combine(rank, back):
    return pl.pallas_call(
        combine_kernel,
        out_shape=jax.ShapeDtypeStruct((rank.shape[1], back.shape[1]), BF16),
        compiler_params=pltpu.CompilerParams(vmem_limit_bytes=16 * 1024 * 1024),
        name="combine_rows",
    )(rank, back)


def swap_halves(x):
    return lax.ppermute(x, "dp", [(d, (d + RING) % (2 * RING)) for d in range(2 * RING)])


def shift_ring(x, by):
    pairs = [(d, d // RING * RING + (d + by) % RING) for d in range(2 * RING)]
    return lax.ppermute(x, "dp", pairs)


def shift_across(x, by):
    pairs = [(d, (d + RING) % (2 * RING) // RING * RING + (d + by) % RING) for d in range(2 * RING)]
    return lax.ppermute(x, "dp", pairs)


def gather_weights(gate_up, down):
    own = jnp.concatenate([gate_up[0], down[0]], axis=1)
    shard = own.shape[0]
    opposite = RING // 2
    other = swap_halves(own)
    far_own, far_other = shift_ring(own, opposite), shift_across(own, opposite)
    both = jnp.concatenate([own, other], axis=0)
    far = jnp.concatenate([far_own, far_other], axis=0)
    ahead, behind = shift_ring(both, 1), shift_ring(both, -1)
    pieces = [both, far, ahead, behind]
    held = [[0], [opposite], [-1], [1]]
    ahead, behind = jnp.concatenate([ahead, far], axis=0), jnp.concatenate([behind, far], axis=0)
    for j in range(2, opposite // 2 + 1):
        ahead, behind = shift_ring(ahead, 1), shift_ring(behind, -1)
        pieces += [ahead, behind]
        held += [[-j, opposite + 1 - j], [j, j - 1 - opposite]]
    plan = [
        (array, (2 * k + part) * shard, offset, part)
        for array, offsets in enumerate(held)
        for k, offset in enumerate(offsets)
        for part in range(2)
    ]
    return pieces, plan


def near_sum_kernel(my_dp, keep_ref, plus_ref, minus_ref, plus2_ref, minus2_ref, later_ref, out_ref):
    del later_ref
    shard = out_ref.shape[1]
    far = (my_dp() % RING) // NEAR
    groups = RING // NEAR
    for j in range(groups):
        value = keep_ref[j].astype(F32) + plus_ref[j].astype(F32) + minus_ref[j].astype(F32)
        target = (far + j) % groups
        out_ref[target] = (value[:shard] + plus2_ref[j].astype(F32)).astype(BF16)
        out_ref[groups + target] = (
            value[shard:] + minus2_ref[(j - 1) % groups].astype(F32)
        ).astype(BF16)


def scatter_sum(keep, plus, minus, plus2, minus2, later, scale, my_dp):
    unit, columns = keep.shape[1:]
    parts = pl.pallas_call(
        functools.partial(near_sum_kernel, my_dp),
        out_shape=jax.ShapeDtypeStruct((2 * RING // NEAR, unit // 2, columns), BF16),
        in_specs=[pl.BlockSpec(memory_space=pltpu.VMEM)] * 5 + [pl.BlockSpec(memory_space=pl.ANY)],
        compiler_params=pltpu.CompilerParams(vmem_limit_bytes=12 * 1024 * 1024),
        name="near_sum",
    )(
        keep,
        shift_ring(plus, 1),
        shift_ring(minus, -1),
        shift_ring(plus2, 2),
        shift_ring(minus2, -2),
        later,
    )
    groups = [
        [y * RING + far * NEAR + near for y in range(2) for far in range(RING // NEAR)]
        for near in range(NEAR)
    ]
    parts = lax.all_to_all(
        parts, "dp", split_axis=0, concat_axis=0, axis_index_groups=groups, tiled=True
    )
    return jnp.sum(parts.astype(F32), axis=0, keepdims=True) * scale


def shards(tokens, cotangent, route_experts, route_weights, gate_up, down):
    rows, features = tokens.shape
    hidden = down.shape[2]
    packed, rank = pack(tokens, cotangent, route_experts, route_weights)
    gathered = lax.all_gather(packed, "expert", axis=0, tiled=True)
    pieces, plan = gather_weights(gate_up, down)

    def my_dp():
        return lax.axis_index("dp")

    row_grads, *grad_parts = expert_work(
        gathered, pieces, plan, features, hidden, lambda: lax.axis_index("expert"), my_dp
    )
    returned = lax.all_to_all(
        row_grads.reshape(EXPERTS, CAP, features), "expert", split_axis=0, concat_axis=0, tiled=True
    )
    grad_scale = 1.0 / math.sqrt(rows * lax.axis_size("dp") * lax.axis_size("expert"))
    grad_gate_up = scatter_sum(*grad_parts, returned, grad_scale, my_dp)
    token_grad = combine(rank, returned.reshape(EXPERTS * CAP, features))
    return (token_grad, grad_gate_up)


def solution(mesh):
    in_specs = (
        P(("dp", "expert"), None),
        P(("dp", "expert"), None),
        P(("dp", "expert"), None),
        P(("dp", "expert"), None),
        P("expert", "dp", None),
        P("expert", "dp", None),
    )
    out_specs = (P(("dp", "expert"), None), P("expert", "dp", None))
    return jax.shard_map(shards, mesh=mesh, in_specs=in_specs, out_specs=out_specs, check_vma=False)
```

```python
import functools
import math

import jax
import jax.numpy as jnp
from jax import lax
from jax.experimental import pallas as pl
from jax.experimental.pallas import tpu as pltpu
from jax.sharding import PartitionSpec as P

EXPERTS = 16
CAP = 80
LANES = 128
RING = 16
NEAR = 4
PAIR = 2
BLOCKS = 4
UNROUTED = 200.0
MIB = 1024 * 1024
VMEM_BYTES = 60 * MIB
HBM = pl.BlockSpec(memory_space=pltpu.HBM)
VMEM = pl.BlockSpec(memory_space=pltpu.VMEM)
BF16 = jnp.bfloat16
F32 = jnp.float32


def iota(shape, dim):
    return lax.broadcasted_iota(jnp.int32, shape, dim)


def as_bf16(mask):
    return jnp.where(mask, 1.0, 0.0).astype(BF16)


def pack_kernel(tok_hbm, cot_hbm, experts_ref, weights_ref, packed_hbm, rank_ref, table_ref, sems):
    rows, features = tok_hbm.shape
    copies = [
        pltpu.make_async_copy(tok_hbm, packed_hbm.at[:, pl.ds(0, features)], sems.at[0]),
        pltpu.make_async_copy(cot_hbm, packed_hbm.at[:, pl.ds(features, features)], sems.at[1]),
        pltpu.make_async_copy(table_ref, packed_hbm.at[:, pl.ds(2 * features, rows)], sems.at[2]),
    ]
    copies[0].start()
    copies[1].start()
    label = iota((EXPERTS, rows), 0)
    dense = jnp.zeros((EXPERTS, rows), F32)
    for k in range(experts_ref.shape[0]):
        dense += jnp.where(experts_ref[k : k + 1, :] == label, weights_ref[k : k + 1, :], 0.0)
    routed = dense > 0.0
    before = as_bf16(iota((rows, rows), 0) < iota((rows, rows), 1))
    rank = jnp.dot(as_bf16(routed), before, preferred_element_type=F32)
    rank = jnp.where(routed, rank, UNROUTED).astype(BF16)
    high = dense.astype(BF16)
    low = (dense - high.astype(F32)).astype(BF16)
    rest = jnp.zeros((rows - 3 * EXPERTS, rows), BF16)
    table_ref[...] = jnp.concatenate([high, low, rank, rest], axis=0)
    copies[2].start()
    rank_ref[...] = rank
    for copy in copies:
        copy.wait()


def pack(tokens, cotangent, route_experts, route_weights):
    rows, features = tokens.shape
    return pl.pallas_call(
        pack_kernel,
        in_specs=[HBM, HBM, VMEM, VMEM],
        out_specs=(HBM, VMEM),
        out_shape=(
            jax.ShapeDtypeStruct((rows, 2 * features + rows), BF16),
            jax.ShapeDtypeStruct((EXPERTS, rows), BF16),
        ),
        scratch_shapes=[pltpu.VMEM((rows, rows), BF16), pltpu.SemaphoreType.DMA((3,))],
        compiler_params=pltpu.CompilerParams(vmem_limit_bytes=VMEM_BYTES),
        name="pack_rows",
    )(tokens, cotangent, route_experts.T, route_weights.T)


def compact_kernel(my_expert, features, g_hbm, inputs_hbm, cots_hbm, blocks, inputs, cots, *sems):
    expert = my_expert()
    pair_total, pair_rows = blocks.shape[:2]
    rows = pair_rows // PAIR
    slots = PAIR * CAP
    loads = [
        pltpu.make_async_copy(
            g_hbm.at[pl.ds(p * pair_rows, pair_rows), :], blocks.at[p], sems[0].at[p]
        )
        for p in range(pair_total)
    ]
    for copy in loads:
        copy.start()
    slot = iota((slots, pair_rows), 0).astype(F32)
    label = iota((3 * EXPERTS, rows), 0)
    stores = []
    for p in range(pair_total):
        loads[p].wait()
        ranks, scales = [], []
        for s in range(PAIR):
            table = blocks[p, s * rows : s * rows + 3 * EXPERTS, 2 * features :].astype(F32)

            def line(k):
                return jnp.sum(
                    jnp.where(label == expert + k * EXPERTS, table, 0.0), axis=0, keepdims=True
                )

            scales.append(line(0) + line(1))
            ranks.append(line(2) + float(s * CAP))
        hit = slot == jnp.concatenate(ranks, axis=1)
        scale = jnp.sum(
            jnp.where(hit, jnp.concatenate(scales, axis=1), 0.0), axis=1, keepdims=True
        )
        pick = as_bf16(hit)
        here = pl.ds(p * slots, slots)
        inputs[here, :] = jnp.dot(
            pick, blocks[p, :, :features], preferred_element_type=F32
        ).astype(BF16)
        cots[here, :] = (
            scale
            * jnp.dot(pick, blocks[p, :, features : 2 * features], preferred_element_type=F32)
        ).astype(BF16)
        stores += [
            pltpu.make_async_copy(inputs.at[here, :], inputs_hbm.at[here, :], sems[1].at[2 * p]),
            pltpu.make_async_copy(cots.at[here, :], cots_hbm.at[here, :], sems[1].at[2 * p + 1]),
        ]
        for copy in stores[-2:]:
            copy.start()
    for copy in stores:
        copy.wait()


def compact(gathered, features, my_expert):
    rows = gathered.shape[0] // EXPERTS
    rows_out = jax.ShapeDtypeStruct((EXPERTS * CAP, features), BF16)
    pairs = EXPERTS // PAIR
    return pl.pallas_call(
        functools.partial(compact_kernel, my_expert, features),
        in_specs=[HBM],
        out_specs=(HBM, HBM),
        out_shape=(rows_out, rows_out),
        scratch_shapes=[
            pltpu.VMEM((pairs, PAIR * rows, gathered.shape[1]), BF16),
            pltpu.VMEM((EXPERTS * CAP, features), BF16),
            pltpu.VMEM((EXPERTS * CAP, features), BF16),
            pltpu.SemaphoreType.DMA((pairs,)),
            pltpu.SemaphoreType.DMA((2 * pairs,)),
        ],
        compiler_params=pltpu.CompilerParams(vmem_limit_bytes=VMEM_BYTES),
        cost_estimate=pl.CostEstimate(
            flops=4 * EXPERTS * CAP * PAIR * rows * features,
            bytes_accessed=16 * MIB,
            transcendentals=0,
        ),
        name="compact_rows",
    )(gathered)


def expert_kernel(my_dp, plan, x_hbm, c_hbm, *refs):
    piece_total = 1 + max(array for array, _, _, _ in plan)
    pieces = refs[:piece_total]
    pre_hbm, gate_up_hbm, *parts_hbm = refs[piece_total : piece_total + 7]
    weights, gate_up, inputs, cots, pre_grad, total, *parts = refs[piece_total + 7 : -4]
    load_sems, weight_sems, pre_sems, out_sems = refs[-4:]
    features, hidden = inputs.shape[1], gate_up.shape[1] // 2
    dp = my_dp()
    upper = dp // RING
    place = dp % RING
    half = features // 2
    shard = half // RING
    block_rows = inputs.shape[0] // BLOCKS

    def rows_of(m):
        return pl.ds(m * block_rows, block_rows)

    def first_row(owner, offset):
        return pl.multiple_of(owner * half + ((place + offset + RING) % RING) * shard, shard)

    loads = []
    for m in range(BLOCKS):
        here = rows_of(m)
        loads += [
            pltpu.make_async_copy(x_hbm.at[here, :], inputs.at[here, :], load_sems.at[2 * m]),
            pltpu.make_async_copy(c_hbm.at[here, :], cots.at[here, :], load_sems.at[2 * m + 1]),
        ]
    weight_loads = []
    for array, source, offset, part in plan:
        owner = upper if part == 0 else 1 - upper
        weight_loads.append(
            pltpu.make_async_copy(
                pieces[array].at[pl.ds(source, shard), :],
                weights.at[pl.ds(first_row(owner, offset), shard), :],
                weight_sems.at[len(weight_loads)],
            )
        )
    for copy in loads[:2] + weight_loads + loads[2:]:
        copy.start()
    for copy in weight_loads:
        copy.wait()
    gate_up[...] = weights[:, : 2 * hidden]
    stores = [pltpu.make_async_copy(gate_up, gate_up_hbm, out_sems.at[0])]
    stores[0].start()
    for m in range(BLOCKS):
        here = rows_of(m)
        loads[2 * m].wait()
        loads[2 * m + 1].wait()
        projected = jnp.dot(inputs[here, :], gate_up[...], preferred_element_type=F32)
        hidden_grad = jnp.dot(cots[here, :], weights[:, 2 * hidden :], preferred_element_type=F32)
        gate_part = projected[:, :hidden]
        up_part = projected[:, hidden:]
        sigmoid_gate = jax.nn.sigmoid(gate_part)
        grad_gate = hidden_grad * up_part * sigmoid_gate * (1.0 + gate_part * (1.0 - sigmoid_gate))
        grad_up = hidden_grad * gate_part * sigmoid_gate
        pre_grad[here, :hidden] = grad_gate.astype(BF16)
        pre_grad[here, hidden:] = grad_up.astype(BF16)
        stores.append(
            pltpu.make_async_copy(pre_grad.at[here, :], pre_hbm.at[here, :], pre_sems.at[m])
        )
        stores[-1].start()

    strip = features // BLOCKS
    for c in range(BLOCKS):
        total[c * strip : (c + 1) * strip, :] = lax.dot_general(
            inputs[:, c * strip : (c + 1) * strip],
            pre_grad[...],
            (((0,), (0,)), ((), ())),
            preferred_element_type=F32,
        )

    def part(owner, offset):
        return total[pl.ds(first_row(owner, offset), shard), :].astype(BF16)

    keep, plus, minus, plus2, minus2 = parts
    for j in range(RING // NEAR):
        for ref, offset in ((keep, 0), (plus, 1), (minus, -1)):
            for owner in range(2):
                ref[j, owner * shard : (owner + 1) * shard, :] = part(owner, NEAR * j + offset)
        plus2[j] = part(0, NEAR * j + 2)
        minus2[j] = part(1, NEAR * j + 2)
    for k, (ref, hbm) in enumerate(zip(parts, parts_hbm)):
        stores.append(pltpu.make_async_copy(ref, hbm, out_sems.at[1 + k]))
        stores[-1].start()
    for copy in stores:
        copy.wait()


def expert_work(inputs, cots, pieces, plan, hidden, my_dp):
    slots, features = inputs.shape
    shard = features // (2 * RING)
    whole = (RING // NEAR, 2 * shard, 2 * hidden)
    half = (RING // NEAR, shard, 2 * hidden)
    parts = [whole, whole, whole, half, half]
    out_shapes = [(slots, 2 * hidden), (features, 2 * hidden)] + parts
    return pl.pallas_call(
        functools.partial(expert_kernel, my_dp, plan),
        in_specs=[HBM] * (2 + len(pieces)),
        out_specs=(HBM,) * len(out_shapes),
        out_shape=tuple(jax.ShapeDtypeStruct(shape, BF16) for shape in out_shapes),
        scratch_shapes=[
            pltpu.VMEM((features, 3 * hidden), BF16),
            pltpu.VMEM((features, 2 * hidden), BF16),
            pltpu.VMEM((slots, features), BF16),
            pltpu.VMEM((slots, features), BF16),
            pltpu.VMEM((slots, 2 * hidden), BF16),
            pltpu.VMEM((features, 2 * hidden), F32),
            *[pltpu.VMEM(shape, BF16) for shape in parts],
            pltpu.SemaphoreType.DMA((2 * BLOCKS,)),
            pltpu.SemaphoreType.DMA((2 * RING,)),
            pltpu.SemaphoreType.DMA((BLOCKS,)),
            pltpu.SemaphoreType.DMA((1 + len(parts),)),
        ],
        compiler_params=pltpu.CompilerParams(vmem_limit_bytes=52 * MIB),
        cost_estimate=pl.CostEstimate(
            flops=5 * slots * features * 2 * hidden,
            bytes_accessed=16 * MIB,
            transcendentals=slots * hidden,
        ),
        name="expert_work",
    )(inputs, cots, *pieces)


def row_kernel(pre_hbm, gate_up_hbm, row_hbm, pre_grad, gate_up, row_grad, sems):
    block = pre_grad.shape[0] // BLOCKS
    loads = [pltpu.make_async_copy(gate_up_hbm, gate_up, sems.at[0])]
    stores = []
    for m in range(BLOCKS):
        here = pl.ds(m * block, block)
        loads.append(
            pltpu.make_async_copy(pre_hbm.at[here, :], pre_grad.at[here, :], sems.at[1 + m])
        )
        stores.append(
            pltpu.make_async_copy(
                row_grad.at[here, :], row_hbm.at[here, :], sems.at[1 + BLOCKS + m]
            )
        )
    for copy in loads:
        copy.start()
    loads[0].wait()
    for m in range(BLOCKS):
        here = pl.ds(m * block, block)
        loads[1 + m].wait()
        row_grad[here, :] = lax.dot_general(
            pre_grad[here, :], gate_up[...], (((1,), (1,)), ((), ())), preferred_element_type=F32
        ).astype(BF16)
        stores[m].start()
    for copy in stores:
        copy.wait()


def row_gradients(pre_grad, gate_up):
    slots, columns = pre_grad.shape
    features = gate_up.shape[0]
    return pl.pallas_call(
        row_kernel,
        in_specs=[HBM, HBM],
        out_specs=HBM,
        out_shape=jax.ShapeDtypeStruct((slots, features), BF16),
        scratch_shapes=[
            pltpu.VMEM((slots, columns), BF16),
            pltpu.VMEM((features, columns), BF16),
            pltpu.VMEM((slots, features), BF16),
            pltpu.SemaphoreType.DMA((1 + 2 * BLOCKS,)),
        ],
        compiler_params=pltpu.CompilerParams(vmem_limit_bytes=VMEM_BYTES),
        cost_estimate=pl.CostEstimate(
            flops=2 * slots * features * columns, bytes_accessed=6 * MIB, transcendentals=0
        ),
        name="row_gradients",
    )(pre_grad, gate_up)


def combine_kernel(rank_ref, back_ref, out_ref):
    slots = back_ref.shape[0]
    column = iota((EXPERTS, slots), 1) - CAP * iota((EXPERTS, slots), 0)
    spread = as_bf16((column >= 0) & (column < CAP))
    rank = lax.dot_general(
        rank_ref[...], spread, (((0,), (0,)), ((), ())), preferred_element_type=F32
    )
    slot = iota((1, slots), 1)
    slot = (slot - CAP * ((slot * 3277) >> 18)).astype(F32)
    pick = as_bf16(rank == slot)
    out_ref[...] = jnp.dot(pick, back_ref[...], preferred_element_type=F32).astype(BF16)


def combine(rank, back):
    return pl.pallas_call(
        combine_kernel,
        out_shape=jax.ShapeDtypeStruct((rank.shape[1], back.shape[1]), BF16),
        compiler_params=pltpu.CompilerParams(vmem_limit_bytes=16 * MIB),
        name="combine_rows",
    )(rank, back)


def swap_halves(x):
    return lax.ppermute(x, "dp", [(d, (d + RING) % (2 * RING)) for d in range(2 * RING)])


def shift_ring(x, by):
    pairs = [(d, d // RING * RING + (d + by) % RING) for d in range(2 * RING)]
    return lax.ppermute(x, "dp", pairs)


def gather_weights(gate_up, down):
    own = jnp.concatenate([gate_up[0], down[0]], axis=1)
    shard = own.shape[0]
    far = [shift_ring(own, -by) for by in range(NEAR, RING, NEAR)]
    base = jnp.concatenate([own, *far], axis=0)
    other = swap_halves(base)
    both = jnp.concatenate([base, other], axis=0)
    pieces = [
        base,
        other,
        shift_ring(both, 1),
        shift_ring(both, -1),
        shift_ring(base, 2),
        shift_ring(other, -2),
    ]
    held = [(0, (0,)), (0, (1,)), (-1, (0, 1)), (1, (0, 1)), (-2, (0,)), (2, (1,))]
    plan = []
    for array, (offset, halves) in enumerate(held):
        for k, part in enumerate(halves):
            for j in range(RING // NEAR):
                row = (k * (RING // NEAR) + j) * shard
                plan.append((array, row, NEAR * j + offset, part))
    return pieces, plan


def near_sum_kernel(my_dp, keep, plus, minus, plus2, minus2, mine, theirs):
    groups, shard = plus2.shape[:2]
    upper = my_dp() // RING
    for j in range(groups):
        value = keep[j].astype(F32) + plus[j].astype(F32) + minus[j].astype(F32)
        low = (value[:shard] + plus2[j].astype(F32)).astype(BF16)
        high = (value[shard:] + minus2[(j - 1) % groups].astype(F32)).astype(BF16)
        mine[j] = jnp.where(upper == 0, low, high)
        theirs[j] = jnp.where(upper == 0, high, low)


def near_sum(my_dp, *parts):
    out = jax.ShapeDtypeStruct(parts[-1].shape, BF16)
    return pl.pallas_call(
        functools.partial(near_sum_kernel, my_dp),
        out_shape=(out, out),
        compiler_params=pltpu.CompilerParams(vmem_limit_bytes=12 * MIB),
        name="near_sum",
    )(*parts)


def scatter_sum(keep, plus, minus, plus2, minus2, scale, my_dp):
    mine, theirs = near_sum(
        my_dp,
        keep,
        shift_ring(plus, 1),
        shift_ring(minus, -1),
        shift_ring(plus2, 2),
        shift_ring(minus2, -2),
    )
    part = (mine.astype(F32) + swap_halves(theirs).astype(F32)).astype(BF16)
    total = part[0].astype(F32)
    for j in range(1, RING // NEAR):
        total += shift_ring(part[j], NEAR * j).astype(F32)
    return (total * scale)[None]


def shards(tokens, cotangent, route_experts, route_weights, gate_up, down):
    rows, features = tokens.shape
    hidden = down.shape[2]
    packed, rank = pack(tokens, cotangent, route_experts, route_weights)
    gathered = lax.all_gather(packed, "expert", axis=0, tiled=True)
    pieces, plan = gather_weights(gate_up, down)

    def my_dp():
        return lax.axis_index("dp")

    inputs, cots = compact(gathered, features, lambda: lax.axis_index("expert"))
    pre_grad, full_gate_up, *grad_parts = expert_work(inputs, cots, pieces, plan, hidden, my_dp)
    row_grads = row_gradients(pre_grad, full_gate_up)
    returned = lax.all_to_all(
        row_grads.reshape(EXPERTS, CAP, features), "expert", split_axis=0, concat_axis=0, tiled=True
    )
    grad_scale = 1.0 / math.sqrt(rows * lax.axis_size("dp") * lax.axis_size("expert"))
    grad_gate_up = scatter_sum(*grad_parts, grad_scale, my_dp)
    token_grad = combine(rank, returned.reshape(EXPERTS * CAP, features))
    return (token_grad, grad_gate_up)


def solution(mesh):
    in_specs = (
        P(("dp", "expert"), None),
        P(("dp", "expert"), None),
        P(("dp", "expert"), None),
        P(("dp", "expert"), None),
        P("expert", "dp", None),
        P("expert", "dp", None),
    )
    out_specs = (P(("dp", "expert"), None), P("expert", "dp", None))
    return jax.shard_map(shards, mesh=mesh, in_specs=in_specs, out_specs=out_specs, check_vma=False)
```

```python
import functools
import math

import jax
import jax.numpy as jnp
from jax import lax
from jax.experimental import pallas as pl
from jax.experimental.pallas import tpu as pltpu
from jax.sharding import PartitionSpec as P

EXPERTS = 16
CAP = 80
LANES = 128
RING = 16
NEAR = 4
PAIR = 2
BLOCKS = 4
UNROUTED = 200.0
MIB = 1024 * 1024
VMEM_BYTES = 60 * MIB
HBM = pl.BlockSpec(memory_space=pltpu.HBM)
VMEM = pl.BlockSpec(memory_space=pltpu.VMEM)
BF16 = jnp.bfloat16
F32 = jnp.float32


def iota(shape, dim):
    return lax.broadcasted_iota(jnp.int32, shape, dim)


def as_bf16(mask):
    return jnp.where(mask, 1.0, 0.0).astype(BF16)


def pack_kernel(tok_ref, cot_ref, experts_ref, weights_ref, packed_ref, rank_ref):
    rows, features = tok_ref.shape
    packed_ref[:, :features] = tok_ref[...]
    packed_ref[:, features : 2 * features] = cot_ref[...]
    label = iota((EXPERTS, rows), 0)
    dense = jnp.zeros((EXPERTS, rows), F32)
    for k in range(experts_ref.shape[0]):
        dense += jnp.where(experts_ref[k : k + 1, :] == label, weights_ref[k : k + 1, :], 0.0)
    routed = dense > 0.0
    before = as_bf16(iota((rows, rows), 0) < iota((rows, rows), 1))
    rank = jnp.dot(as_bf16(routed), before, preferred_element_type=F32)
    rank = jnp.where(routed, rank, UNROUTED).astype(BF16)
    high = dense.astype(BF16)
    low = (dense - high.astype(F32)).astype(BF16)
    rest = jnp.zeros((rows - 3 * EXPERTS, rows), BF16)
    packed_ref[:, 2 * features :] = jnp.concatenate([high, low, rank, rest], axis=0)
    rank_ref[...] = rank


def pack(tokens, cotangent, route_experts, route_weights):
    rows, features = tokens.shape
    return pl.pallas_call(
        pack_kernel,
        out_shape=(
            jax.ShapeDtypeStruct((rows, 2 * features + rows), BF16),
            jax.ShapeDtypeStruct((EXPERTS, rows), BF16),
        ),
        compiler_params=pltpu.CompilerParams(vmem_limit_bytes=VMEM_BYTES),
        name="pack_rows",
    )(tokens, cotangent, route_experts.T, route_weights.T)


def compact_kernel(my_expert, features, g_hbm, inputs_hbm, cots_hbm, blocks, inputs, cots, *sems):
    expert = my_expert()
    pair_total, pair_rows = blocks.shape[:2]
    rows = pair_rows // PAIR
    slots = PAIR * CAP
    loads = [
        pltpu.make_async_copy(
            g_hbm.at[pl.ds(p * pair_rows, pair_rows), :], blocks.at[p], sems[0].at[p]
        )
        for p in range(pair_total)
    ]
    for copy in loads:
        copy.start()
    slot = iota((slots, pair_rows), 0).astype(F32)
    label = iota((3 * EXPERTS, rows), 0)
    stores = []
    for p in range(pair_total):
        loads[p].wait()
        ranks, scales = [], []
        for s in range(PAIR):
            table = blocks[p, s * rows : s * rows + 3 * EXPERTS, 2 * features :].astype(F32)

            def line(k):
                return jnp.sum(
                    jnp.where(label == expert + k * EXPERTS, table, 0.0), axis=0, keepdims=True
                )

            scales.append(line(0) + line(1))
            ranks.append(line(2) + float(s * CAP))
        hit = slot == jnp.concatenate(ranks, axis=1)
        scale = jnp.sum(
            jnp.where(hit, jnp.concatenate(scales, axis=1), 0.0), axis=1, keepdims=True
        )
        pick = as_bf16(hit)
        here = pl.ds(p * slots, slots)
        inputs[here, :] = jnp.dot(
            pick, blocks[p, :, :features], preferred_element_type=F32
        ).astype(BF16)
        cots[here, :] = (
            scale
            * jnp.dot(pick, blocks[p, :, features : 2 * features], preferred_element_type=F32)
        ).astype(BF16)
        stores += [
            pltpu.make_async_copy(inputs.at[here, :], inputs_hbm.at[here, :], sems[1].at[2 * p]),
            pltpu.make_async_copy(cots.at[here, :], cots_hbm.at[here, :], sems[1].at[2 * p + 1]),
        ]
        for copy in stores[-2:]:
            copy.start()
    for copy in stores:
        copy.wait()


def compact(gathered, features, my_expert):
    rows = gathered.shape[0] // EXPERTS
    rows_out = jax.ShapeDtypeStruct((EXPERTS * CAP, features), BF16)
    pairs = EXPERTS // PAIR
    return pl.pallas_call(
        functools.partial(compact_kernel, my_expert, features),
        in_specs=[HBM],
        out_specs=(HBM, HBM),
        out_shape=(rows_out, rows_out),
        scratch_shapes=[
            pltpu.VMEM((pairs, PAIR * rows, gathered.shape[1]), BF16),
            pltpu.VMEM((EXPERTS * CAP, features), BF16),
            pltpu.VMEM((EXPERTS * CAP, features), BF16),
            pltpu.SemaphoreType.DMA((pairs,)),
            pltpu.SemaphoreType.DMA((2 * pairs,)),
        ],
        compiler_params=pltpu.CompilerParams(vmem_limit_bytes=VMEM_BYTES),
        cost_estimate=pl.CostEstimate(
            flops=4 * EXPERTS * CAP * PAIR * rows * features,
            bytes_accessed=16 * MIB,
            transcendentals=0,
        ),
        name="compact_rows",
    )(gathered)


def expert_kernel(my_dp, plan, x_hbm, c_hbm, *refs):
    piece_total = 1 + max(array for array, *_ in plan)
    pieces = refs[:piece_total]
    pre_hbm, gate_up_hbm, *parts_hbm = refs[piece_total : piece_total + 7]
    weights, gate_up, inputs, cots, pre_grad, total, *parts = refs[piece_total + 7 : -4]
    load_sems, weight_sems, pre_sems, out_sems = refs[-4:]
    features, hidden = inputs.shape[1], gate_up.shape[1] // 2
    dp = my_dp()
    upper = dp // RING
    place = dp % RING
    half = features // 2
    shard = half // RING
    block_rows = inputs.shape[0] // BLOCKS

    def rows_of(m):
        return pl.ds(m * block_rows, block_rows)

    def row_at(owner, spot):
        return pl.multiple_of(owner * half + spot * shard, shard)

    loads = []
    for m in range(BLOCKS):
        here = rows_of(m)
        loads += [
            pltpu.make_async_copy(x_hbm.at[here, :], inputs.at[here, :], load_sems.at[2 * m]),
            pltpu.make_async_copy(c_hbm.at[here, :], cots.at[here, :], load_sems.at[2 * m + 1]),
        ]
    weight_loads = []
    for array, source, step, far, part in plan:
        owner = upper if part == 0 else 1 - upper
        spot = NEAR * far + (place + step + NEAR) % NEAR
        weight_loads.append(
            pltpu.make_async_copy(
                pieces[array].at[pl.ds(source, shard), :],
                weights.at[pl.ds(row_at(owner, spot), shard), :],
                weight_sems.at[len(weight_loads)],
            )
        )
    for copy in loads[:2] + weight_loads + loads[2:]:
        copy.start()
    for copy in weight_loads:
        copy.wait()
    gate_up[...] = weights[:, : 2 * hidden]
    stores = [pltpu.make_async_copy(gate_up, gate_up_hbm, out_sems.at[0])]
    stores[0].start()
    for m in range(BLOCKS):
        here = rows_of(m)
        loads[2 * m].wait()
        loads[2 * m + 1].wait()
        projected = jnp.dot(inputs[here, :], gate_up[...], preferred_element_type=F32)
        hidden_grad = jnp.dot(cots[here, :], weights[:, 2 * hidden :], preferred_element_type=F32)
        gate_part = projected[:, :hidden]
        up_part = projected[:, hidden:]
        sigmoid_gate = jax.nn.sigmoid(gate_part)
        grad_gate = hidden_grad * up_part * sigmoid_gate * (1.0 + gate_part * (1.0 - sigmoid_gate))
        grad_up = hidden_grad * gate_part * sigmoid_gate
        pre_grad[here, :hidden] = grad_gate.astype(BF16)
        pre_grad[here, hidden:] = grad_up.astype(BF16)
        stores.append(
            pltpu.make_async_copy(pre_grad.at[here, :], pre_hbm.at[here, :], pre_sems.at[m])
        )
        stores[-1].start()

    strip = features // BLOCKS
    for c in range(BLOCKS):
        total[c * strip : (c + 1) * strip, :] = lax.dot_general(
            inputs[:, c * strip : (c + 1) * strip],
            pre_grad[...],
            (((0,), (0,)), ((), ())),
            preferred_element_type=F32,
        )

    def part(owner, offset):
        return total[pl.ds(row_at(owner, (place + offset + RING) % RING), shard), :].astype(BF16)

    keep, plus, minus, plus2, minus2 = parts
    for j in range(RING // NEAR):
        for ref, offset in ((keep, 0), (plus, 1), (minus, -1)):
            for owner in range(2):
                ref[j, owner * shard : (owner + 1) * shard, :] = part(owner, NEAR * j + offset)
        plus2[j] = part(0, NEAR * j + 2)
        minus2[j] = part(1, NEAR * j + 2)
    for k, (ref, hbm) in enumerate(zip(parts, parts_hbm)):
        stores.append(pltpu.make_async_copy(ref, hbm, out_sems.at[1 + k]))
        stores[-1].start()
    for copy in stores:
        copy.wait()


def expert_work(inputs, cots, pieces, plan, hidden, my_dp):
    slots, features = inputs.shape
    shard = features // (2 * RING)
    whole = (RING // NEAR, 2 * shard, 2 * hidden)
    half = (RING // NEAR, shard, 2 * hidden)
    parts = [whole, whole, whole, half, half]
    out_shapes = [(slots, 2 * hidden), (features, 2 * hidden)] + parts
    return pl.pallas_call(
        functools.partial(expert_kernel, my_dp, plan),
        in_specs=[HBM] * (2 + len(pieces)),
        out_specs=(HBM,) * len(out_shapes),
        out_shape=tuple(jax.ShapeDtypeStruct(shape, BF16) for shape in out_shapes),
        scratch_shapes=[
            pltpu.VMEM((features, 3 * hidden), BF16),
            pltpu.VMEM((features, 2 * hidden), BF16),
            pltpu.VMEM((slots, features), BF16),
            pltpu.VMEM((slots, features), BF16),
            pltpu.VMEM((slots, 2 * hidden), BF16),
            pltpu.VMEM((features, 2 * hidden), F32),
            *[pltpu.VMEM(shape, BF16) for shape in parts],
            pltpu.SemaphoreType.DMA((2 * BLOCKS,)),
            pltpu.SemaphoreType.DMA((2 * RING,)),
            pltpu.SemaphoreType.DMA((BLOCKS,)),
            pltpu.SemaphoreType.DMA((1 + len(parts),)),
        ],
        compiler_params=pltpu.CompilerParams(vmem_limit_bytes=52 * MIB),
        cost_estimate=pl.CostEstimate(
            flops=5 * slots * features * 2 * hidden,
            bytes_accessed=16 * MIB,
            transcendentals=slots * hidden,
        ),
        name="expert_work",
    )(inputs, cots, *pieces)


def row_kernel(pre_hbm, gate_up_hbm, row_hbm, pre_grad, gate_up, row_grad, sems):
    block = pre_grad.shape[0] // BLOCKS
    loads = [pltpu.make_async_copy(gate_up_hbm, gate_up, sems.at[0])]
    stores = []
    for m in range(BLOCKS):
        here = pl.ds(m * block, block)
        loads.append(
            pltpu.make_async_copy(pre_hbm.at[here, :], pre_grad.at[here, :], sems.at[1 + m])
        )
        stores.append(
            pltpu.make_async_copy(
                row_grad.at[here, :], row_hbm.at[here, :], sems.at[1 + BLOCKS + m]
            )
        )
    for copy in loads:
        copy.start()
    loads[0].wait()
    for m in range(BLOCKS):
        here = pl.ds(m * block, block)
        loads[1 + m].wait()
        row_grad[here, :] = lax.dot_general(
            pre_grad[here, :], gate_up[...], (((1,), (1,)), ((), ())), preferred_element_type=F32
        ).astype(BF16)
        stores[m].start()
    for copy in stores:
        copy.wait()


def row_gradients(pre_grad, gate_up):
    slots, columns = pre_grad.shape
    features = gate_up.shape[0]
    return pl.pallas_call(
        row_kernel,
        in_specs=[HBM, HBM],
        out_specs=HBM,
        out_shape=jax.ShapeDtypeStruct((slots, features), BF16),
        scratch_shapes=[
            pltpu.VMEM((slots, columns), BF16),
            pltpu.VMEM((features, columns), BF16),
            pltpu.VMEM((slots, features), BF16),
            pltpu.SemaphoreType.DMA((1 + 2 * BLOCKS,)),
        ],
        compiler_params=pltpu.CompilerParams(vmem_limit_bytes=VMEM_BYTES),
        cost_estimate=pl.CostEstimate(
            flops=2 * slots * features * columns, bytes_accessed=6 * MIB, transcendentals=0
        ),
        name="row_gradients",
    )(pre_grad, gate_up)


def combine_kernel(rank_ref, back_ref, out_ref):
    slots = back_ref.shape[0]
    column = iota((EXPERTS, slots), 1) - CAP * iota((EXPERTS, slots), 0)
    spread = as_bf16((column >= 0) & (column < CAP))
    rank = lax.dot_general(
        rank_ref[...], spread, (((0,), (0,)), ((), ())), preferred_element_type=F32
    )
    slot = iota((1, slots), 1)
    slot = (slot - CAP * ((slot * 3277) >> 18)).astype(F32)
    pick = as_bf16(rank == slot)
    out_ref[...] = jnp.dot(pick, back_ref[...], preferred_element_type=F32).astype(BF16)


def combine(rank, back):
    return pl.pallas_call(
        combine_kernel,
        out_shape=jax.ShapeDtypeStruct((rank.shape[1], back.shape[1]), BF16),
        compiler_params=pltpu.CompilerParams(vmem_limit_bytes=16 * MIB),
        name="combine_rows",
    )(rank, back)


def swap_halves(x):
    return lax.ppermute(x, "dp", [(d, (d + RING) % (2 * RING)) for d in range(2 * RING)])


def shift_ring(x, by):
    pairs = [(d, d // RING * RING + (d + by) % RING) for d in range(2 * RING)]
    return lax.ppermute(x, "dp", pairs)


def far_groups():
    return [
        [y * RING + far * NEAR + near for far in range(RING // NEAR)]
        for y in range(2)
        for near in range(NEAR)
    ]


def gather_weights(gate_up, down):
    own = jnp.concatenate([gate_up[0], down[0]], axis=1)
    shard = own.shape[0]
    both = jnp.concatenate([own, swap_halves(own)], axis=0)
    held = lax.all_gather(both, "dp", axis=0, axis_index_groups=far_groups(), tiled=True)
    middle = held.shape[0] // 2
    pieces = [
        held,
        shift_ring(held, 1),
        shift_ring(held, -1),
        shift_ring(held[:middle], 2),
        shift_ring(held[middle:], -2),
    ]
    groups = RING // NEAR
    everything, first, second = range(groups), range(groups // 2), range(groups // 2, groups)
    steps = [(0, everything), (-1, everything), (1, everything), (2, first), (2, second)]
    plan = [
        (array, (2 * k + part) * shard, step, far, part)
        for array, (step, fars) in enumerate(steps)
        for k, far in enumerate(fars)
        for part in range(2)
    ]
    return pieces, plan


def near_sum_kernel(my_dp, keep, plus, minus, plus2, minus2, mine, theirs):
    groups, shard = plus2.shape[:2]
    upper = my_dp() // RING
    for j in range(groups):
        value = keep[j].astype(F32) + plus[j].astype(F32) + minus[j].astype(F32)
        low = (value[:shard] + plus2[j].astype(F32)).astype(BF16)
        high = (value[shard:] + minus2[(j - 1) % groups].astype(F32)).astype(BF16)
        mine[j] = jnp.where(upper == 0, low, high)
        theirs[j] = jnp.where(upper == 0, high, low)


def near_sum(my_dp, *parts):
    out = jax.ShapeDtypeStruct(parts[-1].shape, BF16)
    return pl.pallas_call(
        functools.partial(near_sum_kernel, my_dp),
        out_shape=(out, out),
        compiler_params=pltpu.CompilerParams(vmem_limit_bytes=12 * MIB),
        cost_estimate=pl.CostEstimate(
            flops=100 * 1000**3, bytes_accessed=4 * MIB, transcendentals=0
        ),
        name="near_sum",
    )(*parts)


def scatter_sum(keep, plus, minus, plus2, minus2, scale, my_dp):
    mine, theirs = near_sum(
        my_dp,
        keep,
        shift_ring(plus, 1),
        shift_ring(minus, -1),
        shift_ring(plus2, 2),
        shift_ring(minus2, -2),
    )
    part = (mine.astype(F32) + swap_halves(theirs).astype(F32)).astype(BF16)
    total = part[0].astype(F32)
    for j in range(1, RING // NEAR):
        total += shift_ring(part[j], NEAR * j).astype(F32)
    return (total * scale)[None]


def shards(tokens, cotangent, route_experts, route_weights, gate_up, down):
    rows, features = tokens.shape
    hidden = down.shape[2]
    packed, rank = pack(tokens, cotangent, route_experts, route_weights)
    gathered = lax.all_gather(packed, "expert", axis=0, tiled=True)
    pieces, plan = gather_weights(gate_up, down)

    def my_dp():
        return lax.axis_index("dp")

    inputs, cots = compact(gathered, features, lambda: lax.axis_index("expert"))
    pre_grad, full_gate_up, *grad_parts = expert_work(inputs, cots, pieces, plan, hidden, my_dp)
    row_grads = row_gradients(pre_grad, full_gate_up)
    returned = lax.all_to_all(
        row_grads.reshape(EXPERTS, CAP, features), "expert", split_axis=0, concat_axis=0, tiled=True
    )
    grad_scale = 1.0 / math.sqrt(rows * lax.axis_size("dp") * lax.axis_size("expert"))
    grad_gate_up = scatter_sum(*grad_parts, grad_scale, my_dp)
    token_grad = combine(rank, returned.reshape(EXPERTS * CAP, features))
    return (token_grad, grad_gate_up)


def solution(mesh):
    in_specs = (
        P(("dp", "expert"), None),
        P(("dp", "expert"), None),
        P(("dp", "expert"), None),
        P(("dp", "expert"), None),
        P("expert", "dp", None),
        P("expert", "dp", None),
    )
    out_specs = (P(("dp", "expert"), None), P("expert", "dp", None))
    return jax.shard_map(shards, mesh=mesh, in_specs=in_specs, out_specs=out_specs, check_vma=False)
```

```python
import functools
import math

import jax
import jax.numpy as jnp
from jax import lax
from jax.experimental import pallas as pl
from jax.experimental.pallas import tpu as pltpu
from jax.sharding import PartitionSpec as P

EXPERTS = 16
CAP = 80
LANES = 128
RING = 16
NEAR = 4
PAIR = 2
BLOCKS = 4
UNROUTED = 200.0
MIB = 1024 * 1024
VMEM_BYTES = 60 * MIB
HBM = pl.BlockSpec(memory_space=pltpu.HBM)
VMEM = pl.BlockSpec(memory_space=pltpu.VMEM)
BF16 = jnp.bfloat16
F32 = jnp.float32


def iota(shape, dim):
    return lax.broadcasted_iota(jnp.int32, shape, dim)


def as_bf16(mask):
    return jnp.where(mask, 1.0, 0.0).astype(BF16)


def pack_kernel(tok_ref, cot_ref, experts_ref, weights_ref, packed_ref, rank_ref):
    rows, features = tok_ref.shape
    packed_ref[:, :features] = tok_ref[...]
    packed_ref[:, features : 2 * features] = cot_ref[...]
    label = iota((EXPERTS, rows), 0)
    dense = jnp.zeros((EXPERTS, rows), F32)
    for k in range(experts_ref.shape[0]):
        dense += jnp.where(experts_ref[k : k + 1, :] == label, weights_ref[k : k + 1, :], 0.0)
    routed = dense > 0.0
    before = as_bf16(iota((rows, rows), 0) < iota((rows, rows), 1))
    rank = jnp.dot(as_bf16(routed), before, preferred_element_type=F32)
    rank = jnp.where(routed, rank, UNROUTED).astype(BF16)
    high = dense.astype(BF16)
    low = (dense - high.astype(F32)).astype(BF16)
    rest = jnp.zeros((rows - 3 * EXPERTS, rows), BF16)
    packed_ref[:, 2 * features :] = jnp.concatenate([high, low, rank, rest], axis=0)
    rank_ref[...] = rank


def pack(tokens, cotangent, route_experts, route_weights):
    rows, features = tokens.shape
    return pl.pallas_call(
        pack_kernel,
        out_shape=(
            jax.ShapeDtypeStruct((rows, 2 * features + rows), BF16),
            jax.ShapeDtypeStruct((EXPERTS, rows), BF16),
        ),
        compiler_params=pltpu.CompilerParams(vmem_limit_bytes=VMEM_BYTES),
        name="pack_rows",
    )(tokens, cotangent, route_experts.T, route_weights.T)


def expert_kernel(my_expert, my_dp, plan, g_hbm, *refs):
    piece_total = 1 + max(array for array, *_ in plan)
    pieces = refs[:piece_total]
    pre_hbm, gate_up_hbm, *parts_hbm = refs[piece_total : piece_total + 7]
    blocks, weights, gate_up, inputs, cots, pre_grad, total, *parts = refs[piece_total + 7 : -4]
    load_sems, weight_sems, pre_sems, out_sems = refs[-4:]
    expert = my_expert()
    features, hidden = inputs.shape[1], gate_up.shape[1] // 2
    dp = my_dp()
    upper = dp // RING
    place = dp % RING
    half = features // 2
    shard = half // RING
    block_rows = inputs.shape[0] // BLOCKS

    def rows_of(m):
        return pl.ds(m * block_rows, block_rows)

    def row_at(owner, spot):
        return pl.multiple_of(owner * half + spot * shard, shard)

    pair_total, pair_rows = blocks.shape[:2]
    rows = pair_rows // PAIR
    loads = [
        pltpu.make_async_copy(
            g_hbm.at[pl.ds(p * pair_rows, pair_rows), :], blocks.at[p], load_sems.at[p]
        )
        for p in range(pair_total)
    ]
    weight_loads = []
    for array, source, step, far, part in plan:
        owner = upper if part == 0 else 1 - upper
        spot = NEAR * far + (place + step + NEAR) % NEAR
        weight_loads.append(
            pltpu.make_async_copy(
                pieces[array].at[pl.ds(source, shard), :],
                weights.at[pl.ds(row_at(owner, spot), shard), :],
                weight_sems.at[len(weight_loads)],
            )
        )
    for copy in loads[:2] + weight_loads + loads[2:]:
        copy.start()
    slot = iota((PAIR * CAP, pair_rows), 0).astype(F32)
    label = iota((3 * EXPERTS, rows), 0)

    def compact(p):
        loads[p].wait()
        ranks, scales = [], []
        for s in range(PAIR):
            table = blocks[p, s * rows : s * rows + 3 * EXPERTS, 2 * features :].astype(F32)

            def line(k):
                return jnp.sum(
                    jnp.where(label == expert + k * EXPERTS, table, 0.0), axis=0, keepdims=True
                )

            scales.append(line(0) + line(1))
            ranks.append(line(2) + float(s * CAP))
        hit = slot == jnp.concatenate(ranks, axis=1)
        scale = jnp.sum(
            jnp.where(hit, jnp.concatenate(scales, axis=1), 0.0), axis=1, keepdims=True
        )
        pick = as_bf16(hit)
        here = pl.ds(p * PAIR * CAP, PAIR * CAP)
        inputs[here, :] = jnp.dot(
            pick, blocks[p, :, :features], preferred_element_type=F32
        ).astype(BF16)
        cots[here, :] = (
            scale
            * jnp.dot(pick, blocks[p, :, features : 2 * features], preferred_element_type=F32)
        ).astype(BF16)

    stores = []
    for m in range(BLOCKS):
        here = rows_of(m)
        for p in range(m * pair_total // BLOCKS, (m + 1) * pair_total // BLOCKS):
            compact(p)
        if m == 0:
            for copy in weight_loads:
                copy.wait()
            gate_up[...] = weights[:, : 2 * hidden]
            stores.append(pltpu.make_async_copy(gate_up, gate_up_hbm, out_sems.at[0]))
            stores[0].start()
        projected = jnp.dot(inputs[here, :], gate_up[...], preferred_element_type=F32)
        hidden_grad = jnp.dot(cots[here, :], weights[:, 2 * hidden :], preferred_element_type=F32)
        gate_part = projected[:, :hidden]
        up_part = projected[:, hidden:]
        sigmoid_gate = jax.nn.sigmoid(gate_part)
        grad_gate = hidden_grad * up_part * sigmoid_gate * (1.0 + gate_part * (1.0 - sigmoid_gate))
        grad_up = hidden_grad * gate_part * sigmoid_gate
        pre_grad[here, :hidden] = grad_gate.astype(BF16)
        pre_grad[here, hidden:] = grad_up.astype(BF16)
        stores.append(
            pltpu.make_async_copy(pre_grad.at[here, :], pre_hbm.at[here, :], pre_sems.at[m])
        )
        stores[-1].start()

    strip = features // BLOCKS
    for c in range(BLOCKS):
        total[c * strip : (c + 1) * strip, :] = lax.dot_general(
            inputs[:, c * strip : (c + 1) * strip],
            pre_grad[...],
            (((0,), (0,)), ((), ())),
            preferred_element_type=F32,
        )

    def part(owner, offset):
        return total[pl.ds(row_at(owner, (place + offset + RING) % RING), shard), :].astype(BF16)

    keep, plus, minus, plus2, minus2 = parts
    for j in range(RING // NEAR):
        for ref, offset in ((keep, 0), (plus, 1), (minus, -1)):
            for owner in range(2):
                ref[j, owner * shard : (owner + 1) * shard, :] = part(owner, NEAR * j + offset)
        plus2[j] = part(0, NEAR * j + 2)
        minus2[j] = part(1, NEAR * j + 2)
    for k, (ref, hbm) in enumerate(zip(parts, parts_hbm)):
        stores.append(pltpu.make_async_copy(ref, hbm, out_sems.at[1 + k]))
        stores[-1].start()
    for copy in stores:
        copy.wait()


def expert_work(gathered, pieces, plan, features, hidden, my_expert, my_dp):
    slots = EXPERTS * CAP
    pair_rows = gathered.shape[0] // EXPERTS * PAIR
    shard = features // (2 * RING)
    whole = (RING // NEAR, 2 * shard, 2 * hidden)
    half = (RING // NEAR, shard, 2 * hidden)
    parts = [whole, whole, whole, half, half]
    out_shapes = [(slots, 2 * hidden), (features, 2 * hidden)] + parts
    return pl.pallas_call(
        functools.partial(expert_kernel, my_expert, my_dp, plan),
        in_specs=[HBM] * (1 + len(pieces)),
        out_specs=(HBM,) * len(out_shapes),
        out_shape=tuple(jax.ShapeDtypeStruct(shape, BF16) for shape in out_shapes),
        scratch_shapes=[
            pltpu.VMEM((EXPERTS // PAIR, pair_rows, gathered.shape[1]), BF16),
            pltpu.VMEM((features, 3 * hidden), BF16),
            pltpu.VMEM((features, 2 * hidden), BF16),
            pltpu.VMEM((slots, features), BF16),
            pltpu.VMEM((slots, features), BF16),
            pltpu.VMEM((slots, 2 * hidden), BF16),
            pltpu.VMEM((features, 2 * hidden), F32),
            *[pltpu.VMEM(shape, BF16) for shape in parts],
            pltpu.SemaphoreType.DMA((EXPERTS // PAIR,)),
            pltpu.SemaphoreType.DMA((2 * RING,)),
            pltpu.SemaphoreType.DMA((BLOCKS,)),
            pltpu.SemaphoreType.DMA((1 + len(parts),)),
        ],
        compiler_params=pltpu.CompilerParams(vmem_limit_bytes=VMEM_BYTES),
        cost_estimate=pl.CostEstimate(
            flops=5 * slots * features * 2 * hidden,
            bytes_accessed=16 * MIB,
            transcendentals=slots * hidden,
        ),
        name="expert_work",
    )(gathered, *pieces)


def row_kernel(pre_hbm, gate_up_hbm, row_hbm, pre_grad, gate_up, row_grad, sems):
    block = pre_grad.shape[0] // BLOCKS
    loads = [pltpu.make_async_copy(gate_up_hbm, gate_up, sems.at[0])]
    stores = []
    for m in range(BLOCKS):
        here = pl.ds(m * block, block)
        loads.append(
            pltpu.make_async_copy(pre_hbm.at[here, :], pre_grad.at[here, :], sems.at[1 + m])
        )
        stores.append(
            pltpu.make_async_copy(
                row_grad.at[here, :], row_hbm.at[here, :], sems.at[1 + BLOCKS + m]
            )
        )
    for copy in loads:
        copy.start()
    loads[0].wait()
    for m in range(BLOCKS):
        here = pl.ds(m * block, block)
        loads[1 + m].wait()
        row_grad[here, :] = lax.dot_general(
            pre_grad[here, :], gate_up[...], (((1,), (1,)), ((), ())), preferred_element_type=F32
        ).astype(BF16)
        stores[m].start()
    for copy in stores:
        copy.wait()


def row_gradients(pre_grad, gate_up):
    slots, columns = pre_grad.shape
    features = gate_up.shape[0]
    return pl.pallas_call(
        row_kernel,
        in_specs=[HBM, HBM],
        out_specs=HBM,
        out_shape=jax.ShapeDtypeStruct((slots, features), BF16),
        scratch_shapes=[
            pltpu.VMEM((slots, columns), BF16),
            pltpu.VMEM((features, columns), BF16),
            pltpu.VMEM((slots, features), BF16),
            pltpu.SemaphoreType.DMA((1 + 2 * BLOCKS,)),
        ],
        compiler_params=pltpu.CompilerParams(vmem_limit_bytes=VMEM_BYTES),
        cost_estimate=pl.CostEstimate(
            flops=2 * slots * features * columns, bytes_accessed=6 * MIB, transcendentals=0
        ),
        name="row_gradients",
    )(pre_grad, gate_up)


def combine_kernel(rank_ref, back_ref, out_ref):
    slots = back_ref.shape[0]
    column = iota((EXPERTS, slots), 1) - CAP * iota((EXPERTS, slots), 0)
    spread = as_bf16((column >= 0) & (column < CAP))
    rank = lax.dot_general(
        rank_ref[...], spread, (((0,), (0,)), ((), ())), preferred_element_type=F32
    )
    slot = iota((1, slots), 1)
    slot = (slot - CAP * ((slot * 3277) >> 18)).astype(F32)
    pick = as_bf16(rank == slot)
    out_ref[...] = jnp.dot(pick, back_ref[...], preferred_element_type=F32).astype(BF16)


def combine(rank, back):
    return pl.pallas_call(
        combine_kernel,
        out_shape=jax.ShapeDtypeStruct((rank.shape[1], back.shape[1]), BF16),
        compiler_params=pltpu.CompilerParams(vmem_limit_bytes=16 * MIB),
        cost_estimate=pl.CostEstimate(
            flops=20 * 1000**3, bytes_accessed=4 * MIB, transcendentals=0
        ),
        name="combine_rows",
    )(rank, back)


def swap_halves(x):
    return lax.ppermute(x, "dp", [(d, (d + RING) % (2 * RING)) for d in range(2 * RING)])


def shift_ring(x, by):
    pairs = [(d, d // RING * RING + (d + by) % RING) for d in range(2 * RING)]
    return lax.ppermute(x, "dp", pairs)


def far_groups():
    return [
        [y * RING + far * NEAR + near for far in range(RING // NEAR)]
        for y in range(2)
        for near in range(NEAR)
    ]


def gather_weights(gate_up, down):
    own = jnp.concatenate([gate_up[0], down[0]], axis=1)
    shard = own.shape[0]
    both = jnp.concatenate([own, swap_halves(own)], axis=0)
    held = lax.all_gather(both, "dp", axis=0, axis_index_groups=far_groups(), tiled=True)
    middle = held.shape[0] // 2
    pieces = [
        held,
        shift_ring(held, 1),
        shift_ring(held, -1),
        shift_ring(held[:middle], 2),
        shift_ring(held[middle:], -2),
    ]
    groups = RING // NEAR
    everything, first, second = range(groups), range(groups // 2), range(groups // 2, groups)
    steps = [(0, everything), (-1, everything), (1, everything), (2, first), (2, second)]
    plan = [
        (array, (2 * k + part) * shard, step, far, part)
        for array, (step, fars) in enumerate(steps)
        for k, far in enumerate(fars)
        for part in range(2)
    ]
    return pieces, plan


def near_sum_kernel(keep, plus, minus, plus2, minus2, out):
    groups, shard = plus2.shape[:2]
    for j in range(groups):
        value = keep[j].astype(F32) + plus[j].astype(F32) + minus[j].astype(F32)
        out[j, :shard] = (value[:shard] + plus2[j].astype(F32)).astype(BF16)
        out[j, shard:] = (value[shard:] + minus2[(j - 1) % groups].astype(F32)).astype(BF16)


def near_sum(*parts):
    return pl.pallas_call(
        near_sum_kernel,
        out_shape=jax.ShapeDtypeStruct(parts[0].shape, BF16),
        compiler_params=pltpu.CompilerParams(vmem_limit_bytes=12 * MIB),
        cost_estimate=pl.CostEstimate(
            flops=100 * 1000**3, bytes_accessed=4 * MIB, transcendentals=0
        ),
        name="near_sum",
    )(*parts)


def far_sum_kernel(my_dp, one, two, three, four, mine, theirs):
    shard = mine.shape[0]
    total = one[...].astype(F32) + two[...].astype(F32) + three[...].astype(F32)
    total += four[...].astype(F32)
    first = my_dp() < RING
    mine[...] = jnp.where(first, total[:shard], total[shard:])
    theirs[...] = jnp.where(first, total[shard:], total[:shard]).astype(BF16)


def far_sum(my_dp, *parts):
    rows, columns = parts[0].shape
    return pl.pallas_call(
        functools.partial(far_sum_kernel, my_dp),
        out_shape=(
            jax.ShapeDtypeStruct((rows // 2, columns), F32),
            jax.ShapeDtypeStruct((rows // 2, columns), BF16),
        ),
        compiler_params=pltpu.CompilerParams(vmem_limit_bytes=12 * MIB),
        name="far_sum",
    )(*parts)


def scatter_sum(keep, plus, minus, plus2, minus2, scale, my_dp):
    part = near_sum(
        keep,
        shift_ring(plus, 1),
        shift_ring(minus, -1),
        shift_ring(plus2, 2),
        shift_ring(minus2, -2),
    )
    parts = [part[0]] + [shift_ring(part[j], NEAR * j) for j in range(1, RING // NEAR)]
    mine, theirs = far_sum(my_dp, *parts)
    return ((mine + swap_halves(theirs).astype(F32)) * scale)[None]


def shards(tokens, cotangent, route_experts, route_weights, gate_up, down):
    rows, features = tokens.shape
    hidden = down.shape[2]
    packed, rank = pack(tokens, cotangent, route_experts, route_weights)
    gathered = lax.all_gather(packed, "expert", axis=0, tiled=True)
    pieces, plan = gather_weights(gate_up, down)

    def my_dp():
        return lax.axis_index("dp")

    pre_grad, full_gate_up, *grad_parts = expert_work(
        gathered, pieces, plan, features, hidden, lambda: lax.axis_index("expert"), my_dp
    )
    row_grads = row_gradients(pre_grad, full_gate_up)
    returned = lax.all_to_all(
        row_grads.reshape(EXPERTS, CAP, features), "expert", split_axis=0, concat_axis=0, tiled=True
    )
    grad_scale = 1.0 / math.sqrt(rows * lax.axis_size("dp") * lax.axis_size("expert"))
    grad_gate_up = scatter_sum(*grad_parts, grad_scale, my_dp)
    token_grad = combine(rank, returned.reshape(EXPERTS * CAP, features))
    return (token_grad, grad_gate_up)


def solution(mesh):
    in_specs = (
        P(("dp", "expert"), None),
        P(("dp", "expert"), None),
        P(("dp", "expert"), None),
        P(("dp", "expert"), None),
        P("expert", "dp", None),
        P("expert", "dp", None),
    )
    out_specs = (P(("dp", "expert"), None), P("expert", "dp", None))
    return jax.shard_map(shards, mesh=mesh, in_specs=in_specs, out_specs=out_specs, check_vma=False)
```

```python
import functools
import math

import jax
import jax.numpy as jnp
from jax import lax
from jax.experimental import pallas as pl
from jax.experimental.pallas import tpu as pltpu
from jax.sharding import PartitionSpec as P

EXPERTS = 16
CAP = 80
LANES = 128
RING = 16
NEAR = 4
PAIR = 2
BLOCKS = 4
UNROUTED = 200.0
MIB = 1024 * 1024
VMEM_BYTES = 60 * MIB
HBM = pl.BlockSpec(memory_space=pltpu.HBM)
VMEM = pl.BlockSpec(memory_space=pltpu.VMEM)
BF16 = jnp.bfloat16
F32 = jnp.float32


def iota(shape, dim):
    return lax.broadcasted_iota(jnp.int32, shape, dim)


def as_bf16(mask):
    return jnp.where(mask, 1.0, 0.0).astype(BF16)


def pack_kernel(tok_ref, cot_ref, experts_ref, weights_ref, packed_ref, rank_ref):
    rows, features = tok_ref.shape
    packed_ref[:, :features] = tok_ref[...]
    packed_ref[:, features : 2 * features] = cot_ref[...]
    label = iota((EXPERTS, rows), 0)
    dense = jnp.zeros((EXPERTS, rows), F32)
    for k in range(experts_ref.shape[0]):
        dense += jnp.where(experts_ref[k : k + 1, :] == label, weights_ref[k : k + 1, :], 0.0)
    routed = dense > 0.0
    before = as_bf16(iota((rows, rows), 0) < iota((rows, rows), 1))
    rank = jnp.dot(as_bf16(routed), before, preferred_element_type=F32)
    rank = jnp.where(routed, rank, UNROUTED).astype(BF16)
    high = dense.astype(BF16)
    low = (dense - high.astype(F32)).astype(BF16)
    rest = jnp.zeros((rows - 3 * EXPERTS, rows), BF16)
    packed_ref[:, 2 * features :] = jnp.concatenate([high, low, rank, rest], axis=0)
    rank_ref[...] = rank


def pack(tokens, cotangent, route_experts, route_weights):
    rows, features = tokens.shape
    return pl.pallas_call(
        pack_kernel,
        out_shape=(
            jax.ShapeDtypeStruct((rows, 2 * features + rows), BF16),
            jax.ShapeDtypeStruct((EXPERTS, rows), BF16),
        ),
        compiler_params=pltpu.CompilerParams(vmem_limit_bytes=VMEM_BYTES),
        name="pack_rows",
    )(tokens, cotangent, route_experts.T, route_weights.T)


def expert_kernel(my_expert, my_dp, plan, g_hbm, *refs):
    piece_total = 1 + max(array for array, *_ in plan)
    pieces = refs[:piece_total]
    pre_hbm, gate_up_hbm, *parts_hbm = refs[piece_total : piece_total + 7]
    blocks, weights, gate_up, inputs, cots, pre_grad, total, *parts = refs[piece_total + 7 : -4]
    load_sems, weight_sems, pre_sems, out_sems = refs[-4:]
    expert = my_expert()
    features, hidden = inputs.shape[1], gate_up.shape[1] // 2
    dp = my_dp()
    upper = dp // RING
    place = dp % RING
    half = features // 2
    shard = half // RING
    block_rows = inputs.shape[0] // BLOCKS

    def rows_of(m):
        return pl.ds(m * block_rows, block_rows)

    def row_at(owner, spot):
        return pl.multiple_of(owner * half + spot * shard, shard)

    pair_total, pair_rows = blocks.shape[:2]
    rows = pair_rows // PAIR
    loads = [
        pltpu.make_async_copy(
            g_hbm.at[pl.ds(p * pair_rows, pair_rows), :], blocks.at[p], load_sems.at[p]
        )
        for p in range(pair_total)
    ]
    weight_loads = []
    for array, source, step, far, part in plan:
        owner = upper if part == 0 else 1 - upper
        spot = NEAR * far + (place + step + NEAR) % NEAR
        weight_loads.append(
            pltpu.make_async_copy(
                pieces[array].at[pl.ds(source, shard), :],
                weights.at[pl.ds(row_at(owner, spot), shard), :],
                weight_sems.at[len(weight_loads)],
            )
        )
    for copy in loads[:2] + weight_loads + loads[2:]:
        copy.start()
    slot = iota((PAIR * CAP, pair_rows), 0).astype(F32)
    label = iota((3 * EXPERTS, rows), 0)

    def compact(p):
        loads[p].wait()
        ranks, scales = [], []
        for s in range(PAIR):
            table = blocks[p, s * rows : s * rows + 3 * EXPERTS, 2 * features :].astype(F32)

            def line(k):
                return jnp.sum(
                    jnp.where(label == expert + k * EXPERTS, table, 0.0), axis=0, keepdims=True
                )

            scales.append(line(0) + line(1))
            ranks.append(line(2) + float(s * CAP))
        hit = slot == jnp.concatenate(ranks, axis=1)
        scale = jnp.sum(
            jnp.where(hit, jnp.concatenate(scales, axis=1), 0.0), axis=1, keepdims=True
        )
        pick = as_bf16(hit)
        here = pl.ds(p * PAIR * CAP, PAIR * CAP)
        inputs[here, :] = jnp.dot(
            pick, blocks[p, :, :features], preferred_element_type=F32
        ).astype(BF16)
        cots[here, :] = (
            scale
            * jnp.dot(pick, blocks[p, :, features : 2 * features], preferred_element_type=F32)
        ).astype(BF16)

    stores = []
    for m in range(BLOCKS):
        here = rows_of(m)
        for p in range(m * pair_total // BLOCKS, (m + 1) * pair_total // BLOCKS):
            compact(p)
        if m == 0:
            for copy in weight_loads:
                copy.wait()
            gate_up[...] = weights[:, : 2 * hidden]
            stores.append(pltpu.make_async_copy(gate_up, gate_up_hbm, out_sems.at[0]))
            stores[0].start()
        projected = jnp.dot(inputs[here, :], gate_up[...], preferred_element_type=F32)
        hidden_grad = jnp.dot(cots[here, :], weights[:, 2 * hidden :], preferred_element_type=F32)
        gate_part = projected[:, :hidden]
        up_part = projected[:, hidden:]
        sigmoid_gate = jax.nn.sigmoid(gate_part)
        grad_gate = hidden_grad * up_part * sigmoid_gate * (1.0 + gate_part * (1.0 - sigmoid_gate))
        grad_up = hidden_grad * gate_part * sigmoid_gate
        pre_grad[here, :hidden] = grad_gate.astype(BF16)
        pre_grad[here, hidden:] = grad_up.astype(BF16)
        stores.append(
            pltpu.make_async_copy(pre_grad.at[here, :], pre_hbm.at[here, :], pre_sems.at[m])
        )
        stores[-1].start()

    strip = features // BLOCKS
    for c in range(BLOCKS):
        total[c * strip : (c + 1) * strip, :] = lax.dot_general(
            inputs[:, c * strip : (c + 1) * strip],
            pre_grad[...],
            (((0,), (0,)), ((), ())),
            preferred_element_type=F32,
        )

    def part(owner, offset):
        return total[pl.ds(row_at(owner, (place + offset + RING) % RING), shard), :].astype(BF16)

    keep, plus, minus, plus2, minus2 = parts
    for j in range(RING // NEAR):
        for ref, offset in ((keep, 0), (plus, 1), (minus, -1)):
            for owner in range(2):
                ref[j, owner * shard : (owner + 1) * shard, :] = part(owner, NEAR * j + offset)
        plus2[j] = part(0, NEAR * j + 2)
        minus2[j] = part(1, NEAR * j + 2)
    for k, (ref, hbm) in enumerate(zip(parts, parts_hbm)):
        stores.append(pltpu.make_async_copy(ref, hbm, out_sems.at[1 + k]))
        stores[-1].start()
    for copy in stores:
        copy.wait()


def expert_work(gathered, pieces, plan, features, hidden, my_expert, my_dp):
    slots = EXPERTS * CAP
    pair_rows = gathered.shape[0] // EXPERTS * PAIR
    shard = features // (2 * RING)
    whole = (RING // NEAR, 2 * shard, 2 * hidden)
    half = (RING // NEAR, shard, 2 * hidden)
    parts = [whole, whole, whole, half, half]
    out_shapes = [(slots, 2 * hidden), (features, 2 * hidden)] + parts
    return pl.pallas_call(
        functools.partial(expert_kernel, my_expert, my_dp, plan),
        in_specs=[HBM] * (1 + len(pieces)),
        out_specs=(HBM,) * len(out_shapes),
        out_shape=tuple(jax.ShapeDtypeStruct(shape, BF16) for shape in out_shapes),
        scratch_shapes=[
            pltpu.VMEM((EXPERTS // PAIR, pair_rows, gathered.shape[1]), BF16),
            pltpu.VMEM((features, 3 * hidden), BF16),
            pltpu.VMEM((features, 2 * hidden), BF16),
            pltpu.VMEM((slots, features), BF16),
            pltpu.VMEM((slots, features), BF16),
            pltpu.VMEM((slots, 2 * hidden), BF16),
            pltpu.VMEM((features, 2 * hidden), F32),
            *[pltpu.VMEM(shape, BF16) for shape in parts],
            pltpu.SemaphoreType.DMA((EXPERTS // PAIR,)),
            pltpu.SemaphoreType.DMA((2 * RING,)),
            pltpu.SemaphoreType.DMA((BLOCKS,)),
            pltpu.SemaphoreType.DMA((1 + len(parts),)),
        ],
        compiler_params=pltpu.CompilerParams(vmem_limit_bytes=VMEM_BYTES),
        cost_estimate=pl.CostEstimate(
            flops=5 * slots * features * 2 * hidden,
            bytes_accessed=16 * MIB,
            transcendentals=slots * hidden,
        ),
        name="expert_work",
    )(gathered, *pieces)


def row_kernel(pre_hbm, gate_up_hbm, row_hbm, pre_grad, gate_up, row_grad, sems):
    block = pre_grad.shape[0] // BLOCKS
    loads = [pltpu.make_async_copy(gate_up_hbm, gate_up, sems.at[0])]
    stores = []
    for m in range(BLOCKS):
        here = pl.ds(m * block, block)
        loads.append(
            pltpu.make_async_copy(pre_hbm.at[here, :], pre_grad.at[here, :], sems.at[1 + m])
        )
        stores.append(
            pltpu.make_async_copy(
                row_grad.at[here, :], row_hbm.at[here, :], sems.at[1 + BLOCKS + m]
            )
        )
    for copy in loads:
        copy.start()
    loads[0].wait()
    for m in range(BLOCKS):
        here = pl.ds(m * block, block)
        loads[1 + m].wait()
        row_grad[here, :] = lax.dot_general(
            pre_grad[here, :], gate_up[...], (((1,), (1,)), ((), ())), preferred_element_type=F32
        ).astype(BF16)
        stores[m].start()
    for copy in stores:
        copy.wait()


def row_gradients(pre_grad, gate_up):
    slots, columns = pre_grad.shape
    features = gate_up.shape[0]
    return pl.pallas_call(
        row_kernel,
        in_specs=[HBM, HBM],
        out_specs=HBM,
        out_shape=jax.ShapeDtypeStruct((slots, features), BF16),
        scratch_shapes=[
            pltpu.VMEM((slots, columns), BF16),
            pltpu.VMEM((features, columns), BF16),
            pltpu.VMEM((slots, features), BF16),
            pltpu.SemaphoreType.DMA((1 + 2 * BLOCKS,)),
        ],
        compiler_params=pltpu.CompilerParams(vmem_limit_bytes=VMEM_BYTES),
        cost_estimate=pl.CostEstimate(
            flops=2 * slots * features * columns, bytes_accessed=6 * MIB, transcendentals=0
        ),
        name="row_gradients",
    )(pre_grad, gate_up)


def combine_kernel(rank_ref, back_ref, out_ref, done_ref):
    done_ref[...] = jnp.zeros_like(done_ref)
    slots = back_ref.shape[0]
    column = iota((EXPERTS, slots), 1) - CAP * iota((EXPERTS, slots), 0)
    spread = as_bf16((column >= 0) & (column < CAP))
    rank = lax.dot_general(
        rank_ref[...], spread, (((0,), (0,)), ((), ())), preferred_element_type=F32
    )
    slot = iota((1, slots), 1)
    slot = (slot - CAP * ((slot * 3277) >> 18)).astype(F32)
    pick = as_bf16(rank == slot)
    out_ref[...] = jnp.dot(pick, back_ref[...], preferred_element_type=F32).astype(BF16)


def combine(rank, back):
    return pl.pallas_call(
        combine_kernel,
        out_shape=(
            jax.ShapeDtypeStruct((rank.shape[1], back.shape[1]), BF16),
            jax.ShapeDtypeStruct((8, LANES), F32),
        ),
        compiler_params=pltpu.CompilerParams(vmem_limit_bytes=16 * MIB),
        cost_estimate=pl.CostEstimate(
            flops=20 * 1000**3, bytes_accessed=4 * MIB, transcendentals=0
        ),
        name="combine_rows",
    )(rank, back)


def swap_halves(x):
    return lax.ppermute(x, "dp", [(d, (d + RING) % (2 * RING)) for d in range(2 * RING)])


def shift_ring(x, by):
    pairs = [(d, d // RING * RING + (d + by) % RING) for d in range(2 * RING)]
    return lax.ppermute(x, "dp", pairs)


def far_groups():
    return [
        [y * RING + far * NEAR + near for far in range(RING // NEAR)]
        for y in range(2)
        for near in range(NEAR)
    ]


def gather_weights(gate_up, down):
    own = jnp.concatenate([gate_up[0], down[0]], axis=1)
    shard = own.shape[0]
    both = jnp.concatenate([own, swap_halves(own)], axis=0)
    held = lax.all_gather(both, "dp", axis=0, axis_index_groups=far_groups(), tiled=True)
    middle = held.shape[0] // 2
    pieces = [
        held,
        shift_ring(held, 1),
        shift_ring(held, -1),
        shift_ring(held[:middle], 2),
        shift_ring(held[middle:], -2),
    ]
    groups = RING // NEAR
    everything, first, second = range(groups), range(groups // 2), range(groups // 2, groups)
    steps = [(0, everything), (-1, everything), (1, everything), (2, first), (2, second)]
    plan = [
        (array, (2 * k + part) * shard, step, far, part)
        for array, (step, fars) in enumerate(steps)
        for k, far in enumerate(fars)
        for part in range(2)
    ]
    return pieces, plan


def near_sum_kernel(keep, plus, minus, plus2, minus2, here, ahead, behind, far_low, far_high):
    groups, shard = plus2.shape[:2]

    def low(j):
        value = keep[j, :shard].astype(F32) + plus[j, :shard].astype(F32)
        return (value + minus[j, :shard].astype(F32) + plus2[j].astype(F32)).astype(BF16)

    def high(j):
        value = keep[j, shard:].astype(F32) + plus[j, shard:].astype(F32)
        value += minus[j, shard:].astype(F32) + minus2[(j - 1) % groups].astype(F32)
        return value.astype(BF16)

    for j, out in ((0, here), (1, ahead), (3, behind)):
        out[:shard] = low(j)
        out[shard:] = high(j)
    far_low[...], far_high[...] = low(2), high(2)


def near_sum(*parts):
    _, rows, columns = parts[0].shape
    whole = jax.ShapeDtypeStruct((rows, columns), BF16)
    half = jax.ShapeDtypeStruct((rows // 2, columns), BF16)
    return pl.pallas_call(
        near_sum_kernel,
        out_shape=(whole, whole, whole, half, half),
        compiler_params=pltpu.CompilerParams(vmem_limit_bytes=12 * MIB),
        cost_estimate=pl.CostEstimate(
            flops=100 * 1000**3, bytes_accessed=4 * MIB, transcendentals=0
        ),
        name="near_sum",
    )(*parts)


def relay_sum_kernel(ahead, behind, got_low, got_high, ahead_out, behind_out):
    shard = got_low.shape[0]
    ahead_out[:shard] = (ahead[:shard].astype(F32) + got_low[...].astype(F32)).astype(BF16)
    ahead_out[shard:] = ahead[shard:]
    behind_out[:shard] = behind[:shard]
    behind_out[shard:] = (behind[shard:].astype(F32) + got_high[...].astype(F32)).astype(BF16)


def relay_sum(ahead, *parts):
    whole = jax.ShapeDtypeStruct(ahead.shape, BF16)
    return pl.pallas_call(
        relay_sum_kernel,
        out_shape=(whole, whole),
        compiler_params=pltpu.CompilerParams(vmem_limit_bytes=12 * MIB),
        name="relay_sum",
    )(ahead, *parts)


def far_sum_kernel(my_dp, here, got_ahead, got_behind, mine, theirs):
    shard = mine.shape[0]
    total = here[...].astype(F32) + got_ahead[...].astype(F32) + got_behind[...].astype(F32)
    first = my_dp() < RING
    mine[...] = jnp.where(first, total[:shard], total[shard:])
    theirs[...] = jnp.where(first, total[shard:], total[:shard]).astype(BF16)


def far_sum(my_dp, *parts):
    rows, columns = parts[0].shape
    return pl.pallas_call(
        functools.partial(far_sum_kernel, my_dp),
        out_shape=(
            jax.ShapeDtypeStruct((rows // 2, columns), F32),
            jax.ShapeDtypeStruct((rows // 2, columns), BF16),
        ),
        compiler_params=pltpu.CompilerParams(vmem_limit_bytes=12 * MIB),
        name="far_sum",
    )(*parts)


def last_sum_kernel(scale, mine, got, earlier, out):
    del earlier
    out[0] = (mine[...] + got[...].astype(F32)) * scale


def last_sum(scale, mine, got, earlier):
    return pl.pallas_call(
        functools.partial(last_sum_kernel, scale),
        in_specs=[VMEM, VMEM, pl.BlockSpec(memory_space=pl.ANY)],
        out_shape=jax.ShapeDtypeStruct((1, *mine.shape), F32),
        compiler_params=pltpu.CompilerParams(vmem_limit_bytes=8 * MIB),
        name="last_sum",
    )(mine, got, earlier)


def scatter_sum(keep, plus, minus, plus2, minus2, my_dp):
    here, ahead, behind, far_low, far_high = near_sum(
        keep,
        shift_ring(plus, 1),
        shift_ring(minus, -1),
        shift_ring(plus2, 2),
        shift_ring(minus2, -2),
    )
    ahead, behind = relay_sum(
        ahead, behind, shift_ring(far_low, NEAR), shift_ring(far_high, -NEAR)
    )
    mine, theirs = far_sum(my_dp, here, shift_ring(ahead, NEAR), shift_ring(behind, -NEAR))
    return mine, swap_halves(theirs)


def shards(tokens, cotangent, route_experts, route_weights, gate_up, down):
    rows, features = tokens.shape
    hidden = down.shape[2]
    packed, rank = pack(tokens, cotangent, route_experts, route_weights)
    gathered = lax.all_gather(packed, "expert", axis=0, tiled=True)
    pieces, plan = gather_weights(gate_up, down)

    def my_dp():
        return lax.axis_index("dp")

    pre_grad, full_gate_up, *grad_parts = expert_work(
        gathered, pieces, plan, features, hidden, lambda: lax.axis_index("expert"), my_dp
    )
    row_grads = row_gradients(pre_grad, full_gate_up)
    returned = lax.all_to_all(
        row_grads.reshape(EXPERTS, CAP, features), "expert", split_axis=0, concat_axis=0, tiled=True
    )
    grad_scale = 1.0 / math.sqrt(rows * lax.axis_size("dp") * lax.axis_size("expert"))
    mine, got = scatter_sum(*grad_parts, my_dp)
    token_grad, done = combine(rank, returned.reshape(EXPERTS * CAP, features))
    grad_gate_up = last_sum(grad_scale, mine, got, done)
    return (token_grad, grad_gate_up)


def solution(mesh):
    in_specs = (
        P(("dp", "expert"), None),
        P(("dp", "expert"), None),
        P(("dp", "expert"), None),
        P(("dp", "expert"), None),
        P("expert", "dp", None),
        P("expert", "dp", None),
    )
    out_specs = (P(("dp", "expert"), None), P("expert", "dp", None))
    return jax.shard_map(shards, mesh=mesh, in_specs=in_specs, out_specs=out_specs, check_vma=False)
```

```python
import functools
import math

import jax
import jax.numpy as jnp
from jax import lax
from jax.experimental import pallas as pl
from jax.experimental.pallas import tpu as pltpu
from jax.sharding import PartitionSpec as P

EXPERTS = 16
CAP = 80
LANES = 128
RING = 16
NEAR = 4
PAIR = 2
BLOCKS = 1
ROW_BLOCKS = 2
STRIPS = 1
UNROUTED = 200.0
MIB = 1024 * 1024
VMEM_BYTES = 60 * MIB
HBM = pl.BlockSpec(memory_space=pltpu.HBM)
VMEM = pl.BlockSpec(memory_space=pltpu.VMEM)
BF16 = jnp.bfloat16
F32 = jnp.float32


def iota(shape, dim):
    return lax.broadcasted_iota(jnp.int32, shape, dim)


def as_bf16(mask):
    return jnp.where(mask, 1.0, 0.0).astype(BF16)


def pack_kernel(tok_ref, cot_ref, experts_ref, weights_ref, packed_ref, rank_ref):
    rows, features = tok_ref.shape
    packed_ref[:, :features] = tok_ref[...]
    packed_ref[:, features : 2 * features] = cot_ref[...]
    label = iota((EXPERTS, rows), 0)
    dense = jnp.zeros((EXPERTS, rows), F32)
    for k in range(experts_ref.shape[0]):
        dense += jnp.where(experts_ref[k : k + 1, :] == label, weights_ref[k : k + 1, :], 0.0)
    routed = dense > 0.0
    before = as_bf16(iota((rows, rows), 0) < iota((rows, rows), 1))
    rank = jnp.dot(as_bf16(routed), before, preferred_element_type=F32)
    rank = jnp.where(routed, rank, UNROUTED).astype(BF16)
    high = dense.astype(BF16)
    low = (dense - high.astype(F32)).astype(BF16)
    rest = jnp.zeros((rows - 3 * EXPERTS, rows), BF16)
    packed_ref[:, 2 * features :] = jnp.concatenate([high, low, rank, rest], axis=0)
    rank_ref[...] = rank


def pack(tokens, cotangent, route_experts, route_weights):
    rows, features = tokens.shape
    return pl.pallas_call(
        pack_kernel,
        out_shape=(
            jax.ShapeDtypeStruct((rows, 2 * features + rows), BF16),
            jax.ShapeDtypeStruct((EXPERTS, rows), BF16),
        ),
        compiler_params=pltpu.CompilerParams(vmem_limit_bytes=VMEM_BYTES),
        name="pack_rows",
    )(tokens, cotangent, route_experts.T, route_weights.T)


def expert_kernel(my_expert, my_dp, plan, g_hbm, *refs):
    piece_total = 1 + max(array for array, *_ in plan)
    pieces = refs[:piece_total]
    pre_hbm, gate_up_hbm, *parts_hbm = refs[piece_total : piece_total + 7]
    blocks, weights, inputs, cots, pre_grad, parts = refs[piece_total + 7 : -4]
    load_sems, weight_sems, pre_sems, out_sems = refs[-4:]
    expert = my_expert()
    features, hidden = inputs.shape[1], pre_grad.shape[1] // 2
    dp = my_dp()
    upper = dp // RING
    place = dp % RING
    half = features // 2
    shard = half // RING
    block_rows = inputs.shape[0] // BLOCKS

    def rows_of(m):
        return pl.ds(m * block_rows, block_rows)

    def row_at(owner, spot):
        return pl.multiple_of(owner * half + spot * shard, shard)

    pair_total, pair_rows = blocks.shape[:2]
    rows = pair_rows // PAIR
    loads = [
        pltpu.make_async_copy(
            g_hbm.at[pl.ds(p * pair_rows, pair_rows), :], blocks.at[p], load_sems.at[p]
        )
        for p in range(pair_total)
    ]
    weight_loads = []
    for array, source, step, far, part in plan:
        owner = upper if part == 0 else 1 - upper
        spot = NEAR * far + (place + step + NEAR) % NEAR
        weight_loads.append(
            pltpu.make_async_copy(
                pieces[array].at[pl.ds(source, shard), :],
                weights.at[pl.ds(row_at(owner, spot), shard), :],
                weight_sems.at[len(weight_loads)],
            )
        )
    for copy in loads[:2] + weight_loads + loads[2:]:
        copy.start()
    slot = iota((PAIR * CAP, pair_rows), 0).astype(F32)
    label = iota((3 * EXPERTS, rows), 0)

    def compact(p):
        loads[p].wait()
        ranks, scales = [], []
        for s in range(PAIR):
            table = blocks[p, s * rows : s * rows + 3 * EXPERTS, 2 * features :].astype(F32)

            def line(k):
                return jnp.sum(
                    jnp.where(label == expert + k * EXPERTS, table, 0.0), axis=0, keepdims=True
                )

            scales.append(line(0) + line(1))
            ranks.append(line(2) + float(s * CAP))
        hit = slot == jnp.concatenate(ranks, axis=1)
        scale = jnp.sum(
            jnp.where(hit, jnp.concatenate(scales, axis=1), 0.0), axis=1, keepdims=True
        )
        pick = as_bf16(hit)
        here = pl.ds(p * PAIR * CAP, PAIR * CAP)
        inputs[here, :] = jnp.dot(
            pick, blocks[p, :, :features], preferred_element_type=F32
        ).astype(BF16)
        cots[here, :] = (
            scale
            * jnp.dot(pick, blocks[p, :, features : 2 * features], preferred_element_type=F32)
        ).astype(BF16)

    stores = []
    for m in range(BLOCKS):
        here = rows_of(m)
        for p in range(m * pair_total // BLOCKS, (m + 1) * pair_total // BLOCKS):
            compact(p)
        if m == 0:
            for copy in weight_loads:
                copy.wait()
            stores.append(
                pltpu.make_async_copy(
                    weights.at[:, pl.ds(0, 2 * hidden)], gate_up_hbm, out_sems.at[0]
                )
            )
            stores[0].start()
        projected = jnp.dot(
            inputs[here, :], weights[:, : 2 * hidden], preferred_element_type=F32
        )
        hidden_grad = jnp.dot(cots[here, :], weights[:, 2 * hidden :], preferred_element_type=F32)
        gate_part = projected[:, :hidden]
        up_part = projected[:, hidden:]
        sigmoid_gate = jax.nn.sigmoid(gate_part)
        grad_gate = hidden_grad * up_part * sigmoid_gate * (1.0 + gate_part * (1.0 - sigmoid_gate))
        grad_up = hidden_grad * gate_part * sigmoid_gate
        pre_grad[here, :hidden] = grad_gate.astype(BF16)
        pre_grad[here, hidden:] = grad_up.astype(BF16)
        stores.append(
            pltpu.make_async_copy(pre_grad.at[here, :], pre_hbm.at[here, :], pre_sems.at[m])
        )
        stores[-1].start()

    strip = features // STRIPS
    for c in range(STRIPS):
        grad = lax.dot_general(
            inputs[:, c * strip : (c + 1) * strip],
            pre_grad[...],
            (((0,), (0,)), ((), ())),
            preferred_element_type=F32,
        ).astype(BF16)
        for k in range(strip // shard):
            owner, spot = divmod(c * strip // shard + k, RING)
            offset = (spot - place + RING) % RING
            kind = offset % NEAR
            kind = jnp.where(kind == 2, 3, jnp.where(kind == 3, 2, kind))
            far = jnp.where(kind == 2, (offset + 1) // NEAR, offset // NEAR) % (RING // NEAR)
            parts[kind, far, owner] = grad[k * shard : (k + 1) * shard]

    sources = [parts.at[k] for k in range(3)] + [parts.at[3, :, half] for half in range(2)]
    for k, (ref, hbm) in enumerate(zip(sources, parts_hbm)):
        stores.append(pltpu.make_async_copy(ref, hbm, out_sems.at[1 + k]))
        stores[-1].start()
    for copy in stores:
        copy.wait()


def expert_work(gathered, pieces, plan, features, hidden, my_expert, my_dp):
    slots = EXPERTS * CAP
    pair_rows = gathered.shape[0] // EXPERTS * PAIR
    shard = features // (2 * RING)
    whole = (RING // NEAR, 2, shard, 2 * hidden)
    half = (RING // NEAR, shard, 2 * hidden)
    parts = [whole, whole, whole, half, half]
    out_shapes = [(slots, 2 * hidden), (features, 2 * hidden)] + parts
    return pl.pallas_call(
        functools.partial(expert_kernel, my_expert, my_dp, plan),
        in_specs=[HBM] * (1 + len(pieces)),
        out_specs=(HBM,) * len(out_shapes),
        out_shape=tuple(jax.ShapeDtypeStruct(shape, BF16) for shape in out_shapes),
        scratch_shapes=[
            pltpu.VMEM((EXPERTS // PAIR, pair_rows, gathered.shape[1]), BF16),
            pltpu.VMEM((features, 3 * hidden), BF16),
            pltpu.VMEM((slots, features), BF16),
            pltpu.VMEM((slots, features), BF16),
            pltpu.VMEM((slots, 2 * hidden), BF16),
            pltpu.VMEM((NEAR, *whole), BF16),
            pltpu.SemaphoreType.DMA((EXPERTS // PAIR,)),
            pltpu.SemaphoreType.DMA((2 * RING,)),
            pltpu.SemaphoreType.DMA((BLOCKS,)),
            pltpu.SemaphoreType.DMA((1 + len(parts),)),
        ],
        compiler_params=pltpu.CompilerParams(vmem_limit_bytes=VMEM_BYTES),
        cost_estimate=pl.CostEstimate(
            flops=5 * slots * features * 2 * hidden,
            bytes_accessed=16 * MIB,
            transcendentals=slots * hidden,
        ),
        name="expert_work",
    )(gathered, *pieces)


def row_kernel(pre_hbm, gate_up_hbm, row_hbm, pre_grad, gate_up, row_grad, sems):
    block = pre_grad.shape[0] // ROW_BLOCKS
    loads = [pltpu.make_async_copy(gate_up_hbm, gate_up, sems.at[0])]
    stores = []
    for m in range(ROW_BLOCKS):
        here = pl.ds(m * block, block)
        loads.append(
            pltpu.make_async_copy(pre_hbm.at[here, :], pre_grad.at[here, :], sems.at[1 + m])
        )
        stores.append(
            pltpu.make_async_copy(
                row_grad.at[here, :], row_hbm.at[here, :], sems.at[1 + ROW_BLOCKS + m]
            )
        )
    for copy in loads:
        copy.start()
    loads[0].wait()
    for m in range(ROW_BLOCKS):
        here = pl.ds(m * block, block)
        loads[1 + m].wait()
        row_grad[here, :] = lax.dot_general(
            pre_grad[here, :], gate_up[...], (((1,), (1,)), ((), ())), preferred_element_type=F32
        ).astype(BF16)
        stores[m].start()
    for copy in stores:
        copy.wait()


def row_gradients(pre_grad, gate_up):
    slots, columns = pre_grad.shape
    features = gate_up.shape[0]
    return pl.pallas_call(
        row_kernel,
        in_specs=[HBM, HBM],
        out_specs=HBM,
        out_shape=jax.ShapeDtypeStruct((slots, features), BF16),
        scratch_shapes=[
            pltpu.VMEM((slots, columns), BF16),
            pltpu.VMEM((features, columns), BF16),
            pltpu.VMEM((slots, features), BF16),
            pltpu.SemaphoreType.DMA((1 + 2 * ROW_BLOCKS,)),
        ],
        compiler_params=pltpu.CompilerParams(vmem_limit_bytes=VMEM_BYTES),
        cost_estimate=pl.CostEstimate(
            flops=2 * slots * features * columns, bytes_accessed=6 * MIB, transcendentals=0
        ),
        name="row_gradients",
    )(pre_grad, gate_up)


def combine_kernel(rank_ref, back_ref, out_ref, done_ref):
    done_ref[...] = jnp.zeros_like(done_ref)
    slots = back_ref.shape[0]
    column = iota((EXPERTS, slots), 1) - CAP * iota((EXPERTS, slots), 0)
    spread = as_bf16((column >= 0) & (column < CAP))
    rank = lax.dot_general(
        rank_ref[...], spread, (((0,), (0,)), ((), ())), preferred_element_type=F32
    )
    slot = iota((1, slots), 1)
    slot = (slot - CAP * ((slot * 3277) >> 18)).astype(F32)
    pick = as_bf16(rank == slot)
    out_ref[...] = jnp.dot(pick, back_ref[...], preferred_element_type=F32).astype(BF16)


def combine(rank, back):
    return pl.pallas_call(
        combine_kernel,
        out_shape=(
            jax.ShapeDtypeStruct((rank.shape[1], back.shape[1]), BF16),
            jax.ShapeDtypeStruct((8, LANES), F32),
        ),
        compiler_params=pltpu.CompilerParams(vmem_limit_bytes=16 * MIB),
        cost_estimate=pl.CostEstimate(
            flops=20 * 1000**3, bytes_accessed=4 * MIB, transcendentals=0
        ),
        name="combine_rows",
    )(rank, back)


def swap_halves(x):
    return lax.ppermute(x, "dp", [(d, (d + RING) % (2 * RING)) for d in range(2 * RING)])


def shift_ring(x, by):
    pairs = [(d, d // RING * RING + (d + by) % RING) for d in range(2 * RING)]
    return lax.ppermute(x, "dp", pairs)


def far_groups():
    return [
        [y * RING + far * NEAR + near for far in range(RING // NEAR)]
        for y in range(2)
        for near in range(NEAR)
    ]


def gather_weights(gate_up, down):
    own = jnp.concatenate([gate_up[0], down[0]], axis=1)
    shard = own.shape[0]
    both = jnp.concatenate([own, swap_halves(own)], axis=0)
    held = lax.all_gather(both, "dp", axis=0, axis_index_groups=far_groups(), tiled=True)
    middle = held.shape[0] // 2
    pieces = [
        held,
        shift_ring(held, 1),
        shift_ring(held, -1),
        shift_ring(held[:middle], 2),
        shift_ring(held[middle:], -2),
    ]
    groups = RING // NEAR
    everything, first, second = range(groups), range(groups // 2), range(groups // 2, groups)
    steps = [(0, everything), (-1, everything), (1, everything), (2, first), (2, second)]
    plan = [
        (array, (2 * k + part) * shard, step, far, part)
        for array, (step, fars) in enumerate(steps)
        for k, far in enumerate(fars)
        for part in range(2)
    ]
    return pieces, plan


def near_sum_kernel(keep, plus, minus, plus2, minus2, *out):
    groups, shard = plus2.shape[:2]
    for j in range(groups):
        value = keep[j].astype(F32) + plus[j].astype(F32) + minus[j].astype(F32)
        out[j][:shard] = (value[:shard] + plus2[j].astype(F32)).astype(BF16)
        out[j][shard:] = (value[shard:] + minus2[(j - 1) % groups].astype(F32)).astype(BF16)


def near_sum(*parts):
    groups, rows, columns = parts[0].shape
    return pl.pallas_call(
        near_sum_kernel,
        out_shape=(jax.ShapeDtypeStruct((rows, columns), BF16),) * groups,
        compiler_params=pltpu.CompilerParams(vmem_limit_bytes=12 * MIB),
        cost_estimate=pl.CostEstimate(
            flops=100 * 1000**3, bytes_accessed=4 * MIB, transcendentals=0
        ),
        name="near_sum",
    )(*parts)


def far_sum_kernel(my_dp, one, two, three, four, mine, theirs):
    shard = mine.shape[0]
    total = one[...].astype(F32) + two[...].astype(F32) + three[...].astype(F32)
    total += four[...].astype(F32)
    first = my_dp() < RING
    mine[...] = jnp.where(first, total[:shard], total[shard:])
    theirs[...] = jnp.where(first, total[shard:], total[:shard]).astype(BF16)


def far_sum(my_dp, *parts):
    rows, columns = parts[0].shape
    return pl.pallas_call(
        functools.partial(far_sum_kernel, my_dp),
        out_shape=(
            jax.ShapeDtypeStruct((rows // 2, columns), F32),
            jax.ShapeDtypeStruct((rows // 2, columns), BF16),
        ),
        compiler_params=pltpu.CompilerParams(vmem_limit_bytes=12 * MIB),
        name="far_sum",
    )(*parts)


def last_sum_kernel(scale, mine, got, earlier, out):
    del earlier
    out[0] = (mine[...] + got[...].astype(F32)) * scale


def last_sum(scale, mine, got, earlier):
    return pl.pallas_call(
        functools.partial(last_sum_kernel, scale),
        in_specs=[VMEM, VMEM, pl.BlockSpec(memory_space=pl.ANY)],
        out_shape=jax.ShapeDtypeStruct((1, *mine.shape), F32),
        compiler_params=pltpu.CompilerParams(vmem_limit_bytes=8 * MIB),
        name="last_sum",
    )(mine, got, earlier)


def scatter_sum(keep, plus, minus, plus2, minus2, my_dp):
    groups, halves, shard, columns = keep.shape
    keep, plus, minus = (x.reshape(groups, halves * shard, columns) for x in (keep, plus, minus))
    parts = near_sum(
        keep,
        shift_ring(plus, 1),
        shift_ring(minus, -1),
        shift_ring(plus2, 2),
        shift_ring(minus2, -2),
    )
    mine, theirs = far_sum(
        my_dp, parts[0], *[shift_ring(parts[j], NEAR * j) for j in range(1, RING // NEAR)]
    )
    return mine, swap_halves(theirs)


def shards(tokens, cotangent, route_experts, route_weights, gate_up, down):
    rows, features = tokens.shape
    hidden = down.shape[2]
    packed, rank = pack(tokens, cotangent, route_experts, route_weights)
    gathered = lax.all_gather(packed, "expert", axis=0, tiled=True)
    pieces, plan = gather_weights(gate_up, down)

    def my_dp():
        return lax.axis_index("dp")

    pre_grad, full_gate_up, *grad_parts = expert_work(
        gathered, pieces, plan, features, hidden, lambda: lax.axis_index("expert"), my_dp
    )
    row_grads = row_gradients(pre_grad, full_gate_up)
    returned = lax.all_to_all(
        row_grads.reshape(EXPERTS, CAP, features), "expert", split_axis=0, concat_axis=0, tiled=True
    )
    grad_scale = 1.0 / math.sqrt(rows * lax.axis_size("dp") * lax.axis_size("expert"))
    mine, got = scatter_sum(*grad_parts, my_dp)
    token_grad, done = combine(rank, returned.reshape(EXPERTS * CAP, features))
    grad_gate_up = last_sum(grad_scale, mine, got, done)
    return (token_grad, grad_gate_up)


def solution(mesh):
    in_specs = (
        P(("dp", "expert"), None),
        P(("dp", "expert"), None),
        P(("dp", "expert"), None),
        P(("dp", "expert"), None),
        P("expert", "dp", None),
        P("expert", "dp", None),
    )
    out_specs = (P(("dp", "expert"), None), P("expert", "dp", None))
    return jax.shard_map(shards, mesh=mesh, in_specs=in_specs, out_specs=out_specs, check_vma=False)
```

```python
import functools
import math

import jax
import jax.numpy as jnp
from jax import lax
from jax.experimental import pallas as pl
from jax.experimental.pallas import tpu as pltpu
from jax.sharding import PartitionSpec as P

EXPERTS = 16
CAP = 80
LANES = 128
RING = 16
NEAR = 4
PAIR = 2
BLOCKS = 1
ROW_BLOCKS = 2
STRIPS = 1
UNROUTED = 200.0
MIB = 1024 * 1024
VMEM_BYTES = 60 * MIB
HBM = pl.BlockSpec(memory_space=pltpu.HBM)
VMEM = pl.BlockSpec(memory_space=pltpu.VMEM)
BF16 = jnp.bfloat16
F32 = jnp.float32


def iota(shape, dim):
    return lax.broadcasted_iota(jnp.int32, shape, dim)


def as_bf16(mask):
    return jnp.where(mask, 1.0, 0.0).astype(BF16)


def pack_kernel(
    tok_ref, cot_ref, experts_ref, weights_ref, gate_up_ref, down_ref, packed_ref, rank_ref, own_ref
):
    rows, features = tok_ref.shape
    own_ref[:, : gate_up_ref.shape[2]] = gate_up_ref[0]
    own_ref[:, gate_up_ref.shape[2] :] = down_ref[0]
    packed_ref[:, :features] = tok_ref[...]
    packed_ref[:, features : 2 * features] = cot_ref[...]
    label = iota((EXPERTS, rows), 0)
    dense = jnp.zeros((EXPERTS, rows), F32)
    for k in range(experts_ref.shape[0]):
        dense += jnp.where(experts_ref[k : k + 1, :] == label, weights_ref[k : k + 1, :], 0.0)
    routed = dense > 0.0
    before = as_bf16(iota((rows, rows), 0) < iota((rows, rows), 1))
    rank = jnp.dot(as_bf16(routed), before, preferred_element_type=F32)
    rank = jnp.where(routed, rank, UNROUTED).astype(BF16)
    high = dense.astype(BF16)
    low = (dense - high.astype(F32)).astype(BF16)
    rest = jnp.zeros((rows - 3 * EXPERTS, rows), BF16)
    packed_ref[:, 2 * features :] = jnp.concatenate([high, low, rank, rest], axis=0)
    rank_ref[...] = rank


def pack(tokens, cotangent, route_experts, route_weights, gate_up, down):
    rows, features = tokens.shape
    return pl.pallas_call(
        pack_kernel,
        out_shape=(
            jax.ShapeDtypeStruct((rows, 2 * features + rows), BF16),
            jax.ShapeDtypeStruct((EXPERTS, rows), BF16),
            jax.ShapeDtypeStruct((gate_up.shape[1], gate_up.shape[2] + down.shape[2]), BF16),
        ),
        compiler_params=pltpu.CompilerParams(vmem_limit_bytes=VMEM_BYTES),
        name="pack_rows",
    )(tokens, cotangent, route_experts.T, route_weights.T, gate_up, down)


def expert_kernel(my_expert, my_dp, plan, g_hbm, *refs):
    piece_total = 1 + max(array for array, *_ in plan)
    pieces = refs[:piece_total]
    pre_hbm, gate_up_hbm, *parts_hbm = refs[piece_total : piece_total + 7]
    blocks, weights, inputs, cots, pre_grad, parts = refs[piece_total + 7 : -4]
    load_sems, weight_sems, pre_sems, out_sems = refs[-4:]
    expert = my_expert()
    features, hidden = inputs.shape[1], pre_grad.shape[1] // 2
    dp = my_dp()
    upper = dp // RING
    place = dp % RING
    half = features // 2
    shard = half // RING
    block_rows = inputs.shape[0] // BLOCKS

    def rows_of(m):
        return pl.ds(m * block_rows, block_rows)

    def row_at(owner, spot):
        return pl.multiple_of(owner * half + spot * shard, shard)

    pair_total, pair_rows = blocks.shape[:2]
    rows = pair_rows // PAIR
    loads = [
        pltpu.make_async_copy(
            g_hbm.at[pl.ds(p * pair_rows, pair_rows), :], blocks.at[p], load_sems.at[p]
        )
        for p in range(pair_total)
    ]
    weight_loads = []
    for array, source, step, far, part in plan:
        owner = upper if part == 0 else 1 - upper
        spot = NEAR * far + (place + step + NEAR) % NEAR
        weight_loads.append(
            pltpu.make_async_copy(
                pieces[array].at[pl.ds(source, shard), :],
                weights.at[pl.ds(row_at(owner, spot), shard), :],
                weight_sems.at[len(weight_loads)],
            )
        )
    for copy in loads[:2] + weight_loads + loads[2:]:
        copy.start()
    slot = iota((PAIR * CAP, pair_rows), 0).astype(F32)
    label = iota((3 * EXPERTS, rows), 0)

    def compact(p):
        loads[p].wait()
        ranks, scales = [], []
        for s in range(PAIR):
            table = blocks[p, s * rows : s * rows + 3 * EXPERTS, 2 * features :].astype(F32)

            def line(k):
                return jnp.sum(
                    jnp.where(label == expert + k * EXPERTS, table, 0.0), axis=0, keepdims=True
                )

            scales.append(line(0) + line(1))
            ranks.append(line(2) + float(s * CAP))
        hit = slot == jnp.concatenate(ranks, axis=1)
        scale = jnp.sum(
            jnp.where(hit, jnp.concatenate(scales, axis=1), 0.0), axis=1, keepdims=True
        )
        pick = as_bf16(hit)
        here = pl.ds(p * PAIR * CAP, PAIR * CAP)
        inputs[here, :] = jnp.dot(
            pick, blocks[p, :, :features], preferred_element_type=F32
        ).astype(BF16)
        cots[here, :] = (
            scale
            * jnp.dot(pick, blocks[p, :, features : 2 * features], preferred_element_type=F32)
        ).astype(BF16)

    stores = []
    for m in range(BLOCKS):
        here = rows_of(m)
        for p in range(m * pair_total // BLOCKS, (m + 1) * pair_total // BLOCKS):
            compact(p)
        if m == 0:
            for copy in weight_loads:
                copy.wait()
            stores.append(
                pltpu.make_async_copy(
                    weights.at[:, pl.ds(0, 2 * hidden)], gate_up_hbm, out_sems.at[0]
                )
            )
            stores[0].start()
        projected = jnp.dot(
            inputs[here, :], weights[:, : 2 * hidden], preferred_element_type=F32
        )
        hidden_grad = jnp.dot(cots[here, :], weights[:, 2 * hidden :], preferred_element_type=F32)
        gate_part = projected[:, :hidden]
        up_part = projected[:, hidden:]
        sigmoid_gate = jax.nn.sigmoid(gate_part)
        grad_gate = hidden_grad * up_part * sigmoid_gate * (1.0 + gate_part * (1.0 - sigmoid_gate))
        grad_up = hidden_grad * gate_part * sigmoid_gate
        pre_grad[here, :hidden] = grad_gate.astype(BF16)
        pre_grad[here, hidden:] = grad_up.astype(BF16)
        stores.append(
            pltpu.make_async_copy(pre_grad.at[here, :], pre_hbm.at[here, :], pre_sems.at[m])
        )
        stores[-1].start()

    strip = features // STRIPS
    for c in range(STRIPS):
        grad = lax.dot_general(
            inputs[:, c * strip : (c + 1) * strip],
            pre_grad[...],
            (((0,), (0,)), ((), ())),
            preferred_element_type=F32,
        ).astype(BF16)
        for k in range(strip // shard):
            owner, spot = divmod(c * strip // shard + k, RING)
            offset = (spot - place + RING) % RING
            kind = offset % NEAR
            kind = jnp.where(kind == 2, 3, jnp.where(kind == 3, 2, kind))
            far = jnp.where(kind == 2, (offset + 1) // NEAR, offset // NEAR) % (RING // NEAR)
            parts[kind, far, owner] = grad[k * shard : (k + 1) * shard]

    sources = [parts.at[k] for k in range(3)] + [parts.at[3, :, half] for half in range(2)]
    for k, (ref, hbm) in enumerate(zip(sources, parts_hbm)):
        stores.append(pltpu.make_async_copy(ref, hbm, out_sems.at[1 + k]))
        stores[-1].start()
    for copy in stores:
        copy.wait()


def expert_work(gathered, pieces, plan, features, hidden, my_expert, my_dp):
    slots = EXPERTS * CAP
    pair_rows = gathered.shape[0] // EXPERTS * PAIR
    shard = features // (2 * RING)
    whole = (RING // NEAR, 2, shard, 2 * hidden)
    half = (RING // NEAR, shard, 2 * hidden)
    parts = [whole, whole, whole, half, half]
    out_shapes = [(slots, 2 * hidden), (features, 2 * hidden)] + parts
    return pl.pallas_call(
        functools.partial(expert_kernel, my_expert, my_dp, plan),
        in_specs=[HBM] * (1 + len(pieces)),
        out_specs=(HBM,) * len(out_shapes),
        out_shape=tuple(jax.ShapeDtypeStruct(shape, BF16) for shape in out_shapes),
        scratch_shapes=[
            pltpu.VMEM((EXPERTS // PAIR, pair_rows, gathered.shape[1]), BF16),
            pltpu.VMEM((features, 3 * hidden), BF16),
            pltpu.VMEM((slots, features), BF16),
            pltpu.VMEM((slots, features), BF16),
            pltpu.VMEM((slots, 2 * hidden), BF16),
            pltpu.VMEM((NEAR, *whole), BF16),
            pltpu.SemaphoreType.DMA((EXPERTS // PAIR,)),
            pltpu.SemaphoreType.DMA((2 * RING,)),
            pltpu.SemaphoreType.DMA((BLOCKS,)),
            pltpu.SemaphoreType.DMA((1 + len(parts),)),
        ],
        compiler_params=pltpu.CompilerParams(vmem_limit_bytes=VMEM_BYTES),
        cost_estimate=pl.CostEstimate(
            flops=5 * slots * features * 2 * hidden,
            bytes_accessed=16 * MIB,
            transcendentals=slots * hidden,
        ),
        name="expert_work",
    )(gathered, *pieces)


def row_kernel(pre_hbm, gate_up_hbm, row_hbm, pre_grad, gate_up, row_grad, sems):
    block = pre_grad.shape[0] // ROW_BLOCKS
    loads = [pltpu.make_async_copy(gate_up_hbm, gate_up, sems.at[0])]
    stores = []
    for m in range(ROW_BLOCKS):
        here = pl.ds(m * block, block)
        loads.append(
            pltpu.make_async_copy(pre_hbm.at[here, :], pre_grad.at[here, :], sems.at[1 + m])
        )
        stores.append(
            pltpu.make_async_copy(
                row_grad.at[here, :], row_hbm.at[here, :], sems.at[1 + ROW_BLOCKS + m]
            )
        )
    for copy in loads:
        copy.start()
    loads[0].wait()
    for m in range(ROW_BLOCKS):
        here = pl.ds(m * block, block)
        loads[1 + m].wait()
        row_grad[here, :] = lax.dot_general(
            pre_grad[here, :], gate_up[...], (((1,), (1,)), ((), ())), preferred_element_type=F32
        ).astype(BF16)
        stores[m].start()
    for copy in stores:
        copy.wait()


def row_gradients(pre_grad, gate_up):
    slots, columns = pre_grad.shape
    features = gate_up.shape[0]
    return pl.pallas_call(
        row_kernel,
        in_specs=[HBM, HBM],
        out_specs=HBM,
        out_shape=jax.ShapeDtypeStruct((slots, features), BF16),
        scratch_shapes=[
            pltpu.VMEM((slots, columns), BF16),
            pltpu.VMEM((features, columns), BF16),
            pltpu.VMEM((slots, features), BF16),
            pltpu.SemaphoreType.DMA((1 + 2 * ROW_BLOCKS,)),
        ],
        compiler_params=pltpu.CompilerParams(vmem_limit_bytes=VMEM_BYTES),
        cost_estimate=pl.CostEstimate(
            flops=2 * slots * features * columns, bytes_accessed=6 * MIB, transcendentals=0
        ),
        name="row_gradients",
    )(pre_grad, gate_up)


def combine_kernel(rank_ref, back_ref, out_ref, done_ref):
    done_ref[...] = jnp.zeros_like(done_ref)
    slots = back_ref.shape[0]
    column = iota((EXPERTS, slots), 1) - CAP * iota((EXPERTS, slots), 0)
    spread = as_bf16((column >= 0) & (column < CAP))
    rank = lax.dot_general(
        rank_ref[...], spread, (((0,), (0,)), ((), ())), preferred_element_type=F32
    )
    slot = iota((1, slots), 1)
    slot = (slot - CAP * ((slot * 3277) >> 18)).astype(F32)
    pick = as_bf16(rank == slot)
    out_ref[...] = jnp.dot(pick, back_ref[...], preferred_element_type=F32).astype(BF16)


def combine(rank, back):
    return pl.pallas_call(
        combine_kernel,
        out_shape=(
            jax.ShapeDtypeStruct((rank.shape[1], back.shape[1]), BF16),
            jax.ShapeDtypeStruct((8, LANES), F32),
        ),
        compiler_params=pltpu.CompilerParams(vmem_limit_bytes=16 * MIB),
        cost_estimate=pl.CostEstimate(
            flops=20 * 1000**3, bytes_accessed=4 * MIB, transcendentals=0
        ),
        name="combine_rows",
    )(rank, back)


def swap_halves(x):
    return lax.ppermute(x, "dp", [(d, (d + RING) % (2 * RING)) for d in range(2 * RING)])


def shift_ring(x, by):
    pairs = [(d, d // RING * RING + (d + by) % RING) for d in range(2 * RING)]
    return lax.ppermute(x, "dp", pairs)


def far_groups():
    return [
        [y * RING + far * NEAR + near for far in range(RING // NEAR)]
        for y in range(2)
        for near in range(NEAR)
    ]


def gather_weights(own):
    shard = own.shape[0]
    both = jnp.concatenate([own, swap_halves(own)], axis=0)
    held = lax.all_gather(both, "dp", axis=0, axis_index_groups=far_groups(), tiled=True)
    middle = held.shape[0] // 2
    pieces = [
        held,
        shift_ring(held, 1),
        shift_ring(held, -1),
        shift_ring(held[:middle], 2),
        shift_ring(held[middle:], -2),
    ]
    groups = RING // NEAR
    everything, first, second = range(groups), range(groups // 2), range(groups // 2, groups)
    steps = [(0, everything), (-1, everything), (1, everything), (2, first), (2, second)]
    plan = [
        (array, (2 * k + part) * shard, step, far, part)
        for array, (step, fars) in enumerate(steps)
        for k, far in enumerate(fars)
        for part in range(2)
    ]
    return pieces, plan


def near_sum_kernel(keep, plus, minus, plus2, minus2, *out):
    groups, shard = plus2.shape[:2]
    for j in range(groups):
        value = keep[j].astype(F32) + plus[j].astype(F32) + minus[j].astype(F32)
        out[j][:shard] = (value[:shard] + plus2[j].astype(F32)).astype(BF16)
        out[j][shard:] = (value[shard:] + minus2[(j - 1) % groups].astype(F32)).astype(BF16)


def near_sum(*parts):
    groups, rows, columns = parts[0].shape
    return pl.pallas_call(
        near_sum_kernel,
        out_shape=(jax.ShapeDtypeStruct((rows, columns), BF16),) * groups,
        compiler_params=pltpu.CompilerParams(vmem_limit_bytes=12 * MIB),
        cost_estimate=pl.CostEstimate(
            flops=100 * 1000**3, bytes_accessed=4 * MIB, transcendentals=0
        ),
        name="near_sum",
    )(*parts)


def far_sum_kernel(my_dp, one, two, three, four, mine, theirs):
    shard = mine.shape[0]
    total = one[...].astype(F32) + two[...].astype(F32) + three[...].astype(F32)
    total += four[...].astype(F32)
    first = my_dp() < RING
    mine[...] = jnp.where(first, total[:shard], total[shard:])
    theirs[...] = jnp.where(first, total[shard:], total[:shard]).astype(BF16)


def far_sum(my_dp, *parts):
    rows, columns = parts[0].shape
    return pl.pallas_call(
        functools.partial(far_sum_kernel, my_dp),
        out_shape=(
            jax.ShapeDtypeStruct((rows // 2, columns), F32),
            jax.ShapeDtypeStruct((rows // 2, columns), BF16),
        ),
        compiler_params=pltpu.CompilerParams(vmem_limit_bytes=12 * MIB),
        name="far_sum",
    )(*parts)


def last_sum_kernel(scale, mine, got, earlier, out):
    del earlier
    out[0] = (mine[...] + got[...].astype(F32)) * scale


def last_sum(scale, mine, got, earlier):
    return pl.pallas_call(
        functools.partial(last_sum_kernel, scale),
        in_specs=[VMEM, VMEM, pl.BlockSpec(memory_space=pl.ANY)],
        out_shape=jax.ShapeDtypeStruct((1, *mine.shape), F32),
        compiler_params=pltpu.CompilerParams(vmem_limit_bytes=8 * MIB),
        name="last_sum",
    )(mine, got, earlier)


def scatter_sum(keep, plus, minus, plus2, minus2, my_dp):
    groups, halves, shard, columns = keep.shape
    keep, plus, minus = (x.reshape(groups, halves * shard, columns) for x in (keep, plus, minus))
    parts = near_sum(
        keep,
        shift_ring(plus, 1),
        shift_ring(minus, -1),
        shift_ring(plus2, 2),
        shift_ring(minus2, -2),
    )
    mine, theirs = far_sum(my_dp, parts[0], *[shift_ring(parts[j], NEAR * j) for j in (2, 1, 3)])
    return mine, swap_halves(theirs)


def shards(tokens, cotangent, route_experts, route_weights, gate_up, down):
    rows, features = tokens.shape
    hidden = down.shape[2]
    packed, rank, own = pack(
        tokens, cotangent, route_experts, route_weights, gate_up, down
    )
    gathered = lax.all_gather(packed, "expert", axis=0, tiled=True)
    pieces, plan = gather_weights(own)

    def my_dp():
        return lax.axis_index("dp")

    pre_grad, full_gate_up, *grad_parts = expert_work(
        gathered, pieces, plan, features, hidden, lambda: lax.axis_index("expert"), my_dp
    )
    row_grads = row_gradients(pre_grad, full_gate_up)
    returned = lax.all_to_all(
        row_grads.reshape(EXPERTS, CAP, features), "expert", split_axis=0, concat_axis=0, tiled=True
    )
    grad_scale = 1.0 / math.sqrt(rows * lax.axis_size("dp") * lax.axis_size("expert"))
    mine, got = scatter_sum(*grad_parts, my_dp)
    token_grad, done = combine(rank, returned.reshape(EXPERTS * CAP, features))
    grad_gate_up = last_sum(grad_scale, mine, got, done)
    return (token_grad, grad_gate_up)


def solution(mesh):
    in_specs = (
        P(("dp", "expert"), None),
        P(("dp", "expert"), None),
        P(("dp", "expert"), None),
        P(("dp", "expert"), None),
        P("expert", "dp", None),
        P("expert", "dp", None),
    )
    out_specs = (P(("dp", "expert"), None), P("expert", "dp", None))
    return jax.shard_map(shards, mesh=mesh, in_specs=in_specs, out_specs=out_specs, check_vma=False)
```

```python
import functools
import math

import jax
import jax.numpy as jnp
from jax import lax
from jax.experimental import pallas as pl
from jax.experimental.pallas import tpu as pltpu
from jax.sharding import PartitionSpec as P

EXPERTS = 16
CAP = 80
LANES = 128
RING = 16
NEAR = 4
PAIR = 2
BLOCKS = 1
STRIPS = 1
UNROUTED = 200.0
MIB = 1024 * 1024
VMEM_BYTES = 60 * MIB
HBM = pl.BlockSpec(memory_space=pltpu.HBM)
VMEM = pl.BlockSpec(memory_space=pltpu.VMEM)
BF16 = jnp.bfloat16
F32 = jnp.float32


def iota(shape, dim):
    return lax.broadcasted_iota(jnp.int32, shape, dim)


def as_bf16(mask):
    return jnp.where(mask, 1.0, 0.0).astype(BF16)


def pack_kernel(
    tok_ref, cot_ref, experts_ref, weights_ref, gate_up_ref, down_ref, packed_ref, rank_ref, own_ref
):
    rows, features = tok_ref.shape
    own_ref[:, : gate_up_ref.shape[2]] = gate_up_ref[0]
    own_ref[:, gate_up_ref.shape[2] :] = down_ref[0]
    packed_ref[:, :features] = tok_ref[...]
    packed_ref[:, features : 2 * features] = cot_ref[...]
    label = iota((EXPERTS, rows), 0)
    dense = jnp.zeros((EXPERTS, rows), F32)
    for k in range(experts_ref.shape[0]):
        dense += jnp.where(experts_ref[k : k + 1, :] == label, weights_ref[k : k + 1, :], 0.0)
    routed = dense > 0.0
    before = as_bf16(iota((rows, rows), 0) < iota((rows, rows), 1))
    rank = jnp.dot(as_bf16(routed), before, preferred_element_type=F32)
    rank = jnp.where(routed, rank, UNROUTED).astype(BF16)
    high = dense.astype(BF16)
    low = (dense - high.astype(F32)).astype(BF16)
    rest = jnp.zeros((rows - 3 * EXPERTS, rows), BF16)
    packed_ref[:, 2 * features :] = jnp.concatenate([high, low, rank, rest], axis=0)
    rank_ref[...] = rank


def pack(tokens, cotangent, route_experts, route_weights, gate_up, down):
    rows, features = tokens.shape
    return pl.pallas_call(
        pack_kernel,
        out_shape=(
            jax.ShapeDtypeStruct((rows, 2 * features + rows), BF16),
            jax.ShapeDtypeStruct((EXPERTS, rows), BF16),
            jax.ShapeDtypeStruct((gate_up.shape[1], gate_up.shape[2] + down.shape[2]), BF16),
        ),
        compiler_params=pltpu.CompilerParams(vmem_limit_bytes=VMEM_BYTES),
        name="pack_rows",
    )(tokens, cotangent, route_experts.T, route_weights.T, gate_up, down)


def expert_kernel(my_expert, my_dp, plan, g_hbm, *refs):
    piece_total = 1 + max(array for array, *_ in plan)
    pieces = refs[:piece_total]
    row_hbm, *parts_hbm = refs[piece_total : piece_total + 6]
    blocks, weights, inputs, cots, pre_grad, row_grad, parts = refs[piece_total + 6 : -4]
    load_sems, weight_sems, pre_sems, out_sems = refs[-4:]
    expert = my_expert()
    features, hidden = inputs.shape[1], pre_grad.shape[1] // 2
    dp = my_dp()
    upper = dp // RING
    place = dp % RING
    half = features // 2
    shard = half // RING
    block_rows = inputs.shape[0] // BLOCKS

    def rows_of(m):
        return pl.ds(m * block_rows, block_rows)

    def row_at(owner, spot):
        return pl.multiple_of(owner * half + spot * shard, shard)

    pair_total, pair_rows = blocks.shape[:2]
    rows = pair_rows // PAIR
    loads = [
        pltpu.make_async_copy(
            g_hbm.at[pl.ds(p * pair_rows, pair_rows), :], blocks.at[p], load_sems.at[p]
        )
        for p in range(pair_total)
    ]
    weight_loads = []
    for array, source, step, far, part in plan:
        owner = upper if part == 0 else 1 - upper
        spot = NEAR * far + (place + step + NEAR) % NEAR
        weight_loads.append(
            pltpu.make_async_copy(
                pieces[array].at[pl.ds(source, shard), :],
                weights.at[pl.ds(row_at(owner, spot), shard), :],
                weight_sems.at[len(weight_loads)],
            )
        )
    for copy in loads[:2] + weight_loads + loads[2:]:
        copy.start()
    slot = iota((PAIR * CAP, pair_rows), 0).astype(F32)
    label = iota((3 * EXPERTS, rows), 0)

    def compact(p):
        loads[p].wait()
        ranks, scales = [], []
        for s in range(PAIR):
            table = blocks[p, s * rows : s * rows + 3 * EXPERTS, 2 * features :].astype(F32)

            def line(k):
                return jnp.sum(
                    jnp.where(label == expert + k * EXPERTS, table, 0.0), axis=0, keepdims=True
                )

            scales.append(line(0) + line(1))
            ranks.append(line(2) + float(s * CAP))
        hit = slot == jnp.concatenate(ranks, axis=1)
        scale = jnp.sum(
            jnp.where(hit, jnp.concatenate(scales, axis=1), 0.0), axis=1, keepdims=True
        )
        pick = as_bf16(hit)
        here = pl.ds(p * PAIR * CAP, PAIR * CAP)
        inputs[here, :] = jnp.dot(
            pick, blocks[p, :, :features], preferred_element_type=F32
        ).astype(BF16)
        cots[here, :] = (
            scale
            * jnp.dot(pick, blocks[p, :, features : 2 * features], preferred_element_type=F32)
        ).astype(BF16)

    stores = []
    for m in range(BLOCKS):
        here = rows_of(m)
        for p in range(m * pair_total // BLOCKS, (m + 1) * pair_total // BLOCKS):
            compact(p)
        if m == 0:
            for copy in weight_loads:
                copy.wait()
        projected = jnp.dot(
            inputs[here, :], weights[:, : 2 * hidden], preferred_element_type=F32
        )
        hidden_grad = jnp.dot(cots[here, :], weights[:, 2 * hidden :], preferred_element_type=F32)
        gate_part = projected[:, :hidden]
        up_part = projected[:, hidden:]
        sigmoid_gate = jax.nn.sigmoid(gate_part)
        grad_gate = hidden_grad * up_part * sigmoid_gate * (1.0 + gate_part * (1.0 - sigmoid_gate))
        grad_up = hidden_grad * gate_part * sigmoid_gate
        pre_grad[here, :hidden] = grad_gate.astype(BF16)
        pre_grad[here, hidden:] = grad_up.astype(BF16)
        row_grad[here, :] = lax.dot_general(
            pre_grad[here, :],
            weights[:, : 2 * hidden],
            (((1,), (1,)), ((), ())),
            preferred_element_type=F32,
        ).astype(BF16)
        stores.append(
            pltpu.make_async_copy(row_grad.at[here, :], row_hbm.at[here, :], pre_sems.at[m])
        )
        stores[-1].start()

    strip = features // STRIPS
    for c in range(STRIPS):
        grad = lax.dot_general(
            inputs[:, c * strip : (c + 1) * strip],
            pre_grad[...],
            (((0,), (0,)), ((), ())),
            preferred_element_type=F32,
        ).astype(BF16)
        for k in range(strip // shard):
            owner, spot = divmod(c * strip // shard + k, RING)
            offset = (spot - place + RING) % RING
            kind = offset % NEAR
            kind = jnp.where(kind == 2, 3, jnp.where(kind == 3, 2, kind))
            far = jnp.where(kind == 2, (offset + 1) // NEAR, offset // NEAR) % (RING // NEAR)
            parts[kind, far, owner] = grad[k * shard : (k + 1) * shard]

    sources = [parts.at[k] for k in range(3)] + [parts.at[3, :, half] for half in range(2)]
    for k, (ref, hbm) in enumerate(zip(sources, parts_hbm)):
        stores.append(pltpu.make_async_copy(ref, hbm, out_sems.at[1 + k]))
        stores[-1].start()
    for copy in stores:
        copy.wait()


def expert_work(gathered, pieces, plan, features, hidden, my_expert, my_dp):
    slots = EXPERTS * CAP
    pair_rows = gathered.shape[0] // EXPERTS * PAIR
    shard = features // (2 * RING)
    whole = (RING // NEAR, 2, shard, 2 * hidden)
    half = (RING // NEAR, shard, 2 * hidden)
    parts = [whole, whole, whole, half, half]
    out_shapes = [(slots, features)] + parts
    return pl.pallas_call(
        functools.partial(expert_kernel, my_expert, my_dp, plan),
        in_specs=[HBM] * (1 + len(pieces)),
        out_specs=(HBM,) * len(out_shapes),
        out_shape=tuple(jax.ShapeDtypeStruct(shape, BF16) for shape in out_shapes),
        scratch_shapes=[
            pltpu.VMEM((EXPERTS // PAIR, pair_rows, gathered.shape[1]), BF16),
            pltpu.VMEM((features, 3 * hidden), BF16),
            pltpu.VMEM((slots, features), BF16),
            pltpu.VMEM((slots, features), BF16),
            pltpu.VMEM((slots, 2 * hidden), BF16),
            pltpu.VMEM((slots, features), BF16),
            pltpu.VMEM((NEAR, *whole), BF16),
            pltpu.SemaphoreType.DMA((EXPERTS // PAIR,)),
            pltpu.SemaphoreType.DMA((2 * RING,)),
            pltpu.SemaphoreType.DMA((BLOCKS,)),
            pltpu.SemaphoreType.DMA((1 + len(parts),)),
        ],
        compiler_params=pltpu.CompilerParams(vmem_limit_bytes=VMEM_BYTES),
        cost_estimate=pl.CostEstimate(
            flops=7 * slots * features * 2 * hidden,
            bytes_accessed=16 * MIB,
            transcendentals=slots * hidden,
        ),
        name="expert_work",
    )(gathered, *pieces)


def combine_kernel(rank_ref, back_ref, out_ref, done_ref):
    done_ref[...] = jnp.zeros_like(done_ref)
    slots = back_ref.shape[0]
    column = iota((EXPERTS, slots), 1) - CAP * iota((EXPERTS, slots), 0)
    spread = as_bf16((column >= 0) & (column < CAP))
    rank = lax.dot_general(
        rank_ref[...], spread, (((0,), (0,)), ((), ())), preferred_element_type=F32
    )
    slot = iota((1, slots), 1)
    slot = (slot - CAP * ((slot * 3277) >> 18)).astype(F32)
    pick = as_bf16(rank == slot)
    out_ref[...] = jnp.dot(pick, back_ref[...], preferred_element_type=F32).astype(BF16)


def combine(rank, back):
    return pl.pallas_call(
        combine_kernel,
        out_shape=(
            jax.ShapeDtypeStruct((rank.shape[1], back.shape[1]), BF16),
            jax.ShapeDtypeStruct((8, LANES), F32),
        ),
        compiler_params=pltpu.CompilerParams(vmem_limit_bytes=16 * MIB),
        cost_estimate=pl.CostEstimate(
            flops=20 * 1000**3, bytes_accessed=4 * MIB, transcendentals=0
        ),
        name="combine_rows",
    )(rank, back)


def swap_halves(x):
    return lax.ppermute(x, "dp", [(d, (d + RING) % (2 * RING)) for d in range(2 * RING)])


def shift_ring(x, by):
    pairs = [(d, d // RING * RING + (d + by) % RING) for d in range(2 * RING)]
    return lax.ppermute(x, "dp", pairs)


def far_groups():
    return [
        [y * RING + far * NEAR + near for far in range(RING // NEAR)]
        for y in range(2)
        for near in range(NEAR)
    ]


def gather_weights(own):
    shard = own.shape[0]
    both = jnp.concatenate([own, swap_halves(own)], axis=0)
    held = lax.all_gather(both, "dp", axis=0, axis_index_groups=far_groups(), tiled=True)
    middle = held.shape[0] // 2
    pieces = [
        held,
        shift_ring(held, 1),
        shift_ring(held, -1),
        shift_ring(held[:middle], 2),
        shift_ring(held[middle:], -2),
    ]
    groups = RING // NEAR
    everything, first, second = range(groups), range(groups // 2), range(groups // 2, groups)
    steps = [(0, everything), (-1, everything), (1, everything), (2, first), (2, second)]
    plan = [
        (array, (2 * k + part) * shard, step, far, part)
        for array, (step, fars) in enumerate(steps)
        for k, far in enumerate(fars)
        for part in range(2)
    ]
    return pieces, plan


def near_sum_kernel(keep, plus, minus, plus2, minus2, *out):
    groups, shard = plus2.shape[:2]
    for j in range(groups):
        value = keep[j].astype(F32) + plus[j].astype(F32) + minus[j].astype(F32)
        out[j][:shard] = (value[:shard] + plus2[j].astype(F32)).astype(BF16)
        out[j][shard:] = (value[shard:] + minus2[(j - 1) % groups].astype(F32)).astype(BF16)


def near_sum(*parts):
    groups, rows, columns = parts[0].shape
    return pl.pallas_call(
        near_sum_kernel,
        out_shape=(jax.ShapeDtypeStruct((rows, columns), BF16),) * groups,
        compiler_params=pltpu.CompilerParams(vmem_limit_bytes=12 * MIB),
        cost_estimate=pl.CostEstimate(
            flops=100 * 1000**3, bytes_accessed=4 * MIB, transcendentals=0
        ),
        name="near_sum",
    )(*parts)


def far_sum_kernel(my_dp, one, two, three, four, mine, theirs):
    shard = mine.shape[0]
    total = one[...].astype(F32) + two[...].astype(F32) + three[...].astype(F32)
    total += four[...].astype(F32)
    first = my_dp() < RING
    mine[...] = jnp.where(first, total[:shard], total[shard:])
    theirs[...] = jnp.where(first, total[shard:], total[:shard]).astype(BF16)


def far_sum(my_dp, *parts):
    rows, columns = parts[0].shape
    return pl.pallas_call(
        functools.partial(far_sum_kernel, my_dp),
        out_shape=(
            jax.ShapeDtypeStruct((rows // 2, columns), F32),
            jax.ShapeDtypeStruct((rows // 2, columns), BF16),
        ),
        compiler_params=pltpu.CompilerParams(vmem_limit_bytes=12 * MIB),
        name="far_sum",
    )(*parts)


def last_sum_kernel(scale, mine, got, earlier, out):
    del earlier
    out[0] = (mine[...] + got[...].astype(F32)) * scale


def last_sum(scale, mine, got, earlier):
    return pl.pallas_call(
        functools.partial(last_sum_kernel, scale),
        in_specs=[VMEM, VMEM, pl.BlockSpec(memory_space=pl.ANY)],
        out_shape=jax.ShapeDtypeStruct((1, *mine.shape), F32),
        compiler_params=pltpu.CompilerParams(vmem_limit_bytes=8 * MIB),
        name="last_sum",
    )(mine, got, earlier)


def scatter_sum(keep, plus, minus, plus2, minus2, my_dp):
    groups, halves, shard, columns = keep.shape
    keep, plus, minus = (x.reshape(groups, halves * shard, columns) for x in (keep, plus, minus))
    parts = near_sum(
        keep,
        shift_ring(plus, 1),
        shift_ring(minus, -1),
        shift_ring(plus2, 2),
        shift_ring(minus2, -2),
    )
    mine, theirs = far_sum(my_dp, parts[0], *[shift_ring(parts[j], NEAR * j) for j in (2, 1, 3)])
    return mine, swap_halves(theirs)


def shards(tokens, cotangent, route_experts, route_weights, gate_up, down):
    rows, features = tokens.shape
    hidden = down.shape[2]
    packed, rank, own = pack(
        tokens, cotangent, route_experts, route_weights, gate_up, down
    )
    gathered = lax.all_gather(packed, "expert", axis=0, tiled=True)
    pieces, plan = gather_weights(own)

    def my_dp():
        return lax.axis_index("dp")

    row_grads, *grad_parts = expert_work(
        gathered, pieces, plan, features, hidden, lambda: lax.axis_index("expert"), my_dp
    )
    returned = lax.all_to_all(
        row_grads.reshape(EXPERTS, CAP, features), "expert", split_axis=0, concat_axis=0, tiled=True
    )
    grad_scale = 1.0 / math.sqrt(rows * lax.axis_size("dp") * lax.axis_size("expert"))
    mine, got = scatter_sum(*grad_parts, my_dp)
    token_grad, done = combine(rank, returned.reshape(EXPERTS * CAP, features))
    grad_gate_up = last_sum(grad_scale, mine, got, done)
    return (token_grad, grad_gate_up)


def solution(mesh):
    in_specs = (
        P(("dp", "expert"), None),
        P(("dp", "expert"), None),
        P(("dp", "expert"), None),
        P(("dp", "expert"), None),
        P("expert", "dp", None),
        P("expert", "dp", None),
    )
    out_specs = (P(("dp", "expert"), None), P("expert", "dp", None))
    return jax.shard_map(shards, mesh=mesh, in_specs=in_specs, out_specs=out_specs, check_vma=False)
```
